256 devices in a mesh: slab: 32 (over x, z_lo, core), kgrp: 8 (over y, z_hi).
Axes of the slice: x: 4, y: 4, z: 8 (z_hi: 2, z_lo: 4; z = z_hi * 4 + z_lo), core: 2. Of those that a mesh axis runs over, the one named last changes fastest.
Arguments:
- atom_descriptors: bfloat16 [32768, 128], P(('slab', 'kgrp')), may hold values from -6 to 6
- atom_locations: float32 [3, 32768], P(None, ('slab', 'kgrp')), may hold values from 0 to 32, as said below
- adjacent_atom_slots: int32 [32768, 64], P(('slab', 'kgrp')), may hold values from 0 to 3071
- neighbour_tally: int32 [32768], P(('slab', 'kgrp')), may hold values from 16 to 64
- filled_slot_tallies: int32 [32], replicated, may hold values from 1 to 1024, 24576 in all
- reciprocal_lattice_modes: float32 [3, 8192], P(None, 'kgrp'), may hold values from -4 to 4
- edge_update_matrix: bfloat16 [2, 128, 128], replicated, may hold values from -0.5 to 0.5
- node_update_matrix: bfloat16 [2, 128, 128], replicated, may hold values from -0.5 to 0.5
- distance_basis_mixing: float32 [2, 8, 128], replicated, may hold values from -2 to 2
- latent_ionic_readout: bfloat16 [128, 16], replicated, may hold values from -0.5 to 0.5
Outputs:
- potential: float32 [16, 32768], P(None, ('slab', 'kgrp'))
- forces: float32 [3, 32768], P(None, ('slab', 'kgrp'))
The draws below stay inside these ranges and needn't reach their ends.
Inputs may be any that keep to these rules, and one draw needn't show every extreme that they name: `atom_locations`: coordinates of atoms of slab s: first in [s, s+1), others in [0, 1).
All inputs are finite; a program needn't handle non-finite values.
Results may differ from the reference program's by a relative error of at most 0.0028.
Values may be sent and summed in bfloat16 or wider, within the bound.
No kernel may reach another device: no remote copies, remote signals or barrier semaphores. Data moves between devices by JAX's collectives and lax.ppermute only.
A program may use at most 64 MiB of HBM per device.

```python
import math
import jax
import jax.numpy as jnp
import numpy as np
from jax import lax

C = 128
LATENT = 16
RECIP_MODES = 8192
NEIGH = 64
NB = 8
LAYERS = 2
SLAB_ATOMS = 1024
ATOMS = 32768
N_SLAB = 32


def draw_atom_locations(key, part):
    key = jax.random.fold_in(key, 11)
    uniform_values = jax.random.uniform(key, (3, ATOMS), jnp.float32)
    fraction = uniform_values
    slab_offset = (jnp.arange(ATOMS) // SLAB_ATOMS).astype(jnp.float32)
    return jnp.stack([fraction[0] + slab_offset, fraction[1], fraction[2]])


def place_ends(values, stream_key, smallest, high):
    spot = [jax.random.randint(jax.random.fold_in(stream_key, axis), (), 0, length) for axis, length in enumerate(values.shape)]
    longest = values.shape.index(max(values.shape))
    beside = spot[:longest] + [(spot[longest] + 1) % values.shape[longest]] + spot[longest + 1:]
    return values.at[tuple(spot)].set(smallest).at[tuple(beside)].set(high)


def block_scale(own_key, extent, shards, smallest, largest):
    loudness, own = 1.0, jax.random.fold_in(own_key, 6)
    for position, parts in shards:
        draws = jnp.exp(jax.random.uniform(jax.random.fold_in(own, position), (parts,), jnp.float32, smallest / len(shards), largest / len(shards)))
        loudness = loudness * jnp.repeat(draws, extent[position] // parts).reshape([-1 if axis == position else 1 for axis in range(len(extent))])
    return loudness


def profile(amount, total, bound, slope):
    portions = [(1 << 20) // math.isqrt(grade ** slope) + 1 for grade in range(2, amount + 1)]
    surplus, holding = total - bound - (amount - 1), [1] * (amount - 1)
    while surplus > 0:
        free = [i for i in range(amount - 1) if holding[i] < bound]
        mass, budget = sum([portions[i] for i in free]), surplus
        for i in free:
            more = min(bound - holding[i], max(1, budget * portions[i] // mass), surplus)
            holding[i] = holding[i] + more
            surplus = surplus - more
    return np.array([bound] + holding)


def uneven(own_key, amount, total, reach, skew):
    if amount == 2:
        one = jax.random.randint(own_key, (), max(1, total - reach), min(reach, total - 1) + 1)
        return jnp.stack([one, total - one])
    tallies = jnp.asarray(profile(amount, total, reach, skew), jnp.int32)
    twos = (amount - 1) // 2
    source_of, sink = tallies[1:1 + 2 * twos:2], tallies[2:2 + 2 * twos:2]
    margin = jnp.minimum(source_of - 1, reach - sink)
    moved = jax.random.randint(jax.random.fold_in(own_key, 1), (twos,), 0, 1 << 20) % (margin + 1)
    tallies = tallies.at[1:1 + 2 * twos:2].set(source_of - moved).at[2:2 + 2 * twos:2].set(sink + moved)
    return tallies[jax.random.permutation(jax.random.fold_in(own_key, 2), amount)]


def centred(key, shape, spread, bound, cuts=(), kind=jnp.bfloat16):
    drawn = spread * jax.random.normal(key, shape, jnp.float32)
    if cuts:
        drawn = drawn * block_scale(key, shape, cuts, -0.22, 0.18)
    return jnp.clip(drawn, -bound, bound).astype(kind)


def setup_inputs(seed: int = 0) -> dict:
    splits = jax.random.split(jax.random.key(seed), 11)
    return {
        "atom_descriptors": centred(splits[0], (ATOMS, C), 1.0, 6.0, ((0, 256),)),
        "atom_locations": draw_atom_locations(jax.random.fold_in(splits[10], 71), 0),
        "adjacent_atom_slots": place_ends(jax.random.randint(splits[2], (ATOMS, NEIGH), 0, 3 * SLAB_ATOMS), jax.random.fold_in(splits[2], 1), 0, (3 * SLAB_ATOMS) - 1).astype(jnp.int32),
        "neighbour_tally": place_ends(jax.random.randint(splits[3], (ATOMS,), 16, NEIGH + 1), jax.random.fold_in(splits[3], 1), 16, NEIGH).astype(jnp.int32),
        "filled_slot_tallies": uneven(splits[4], N_SLAB, N_SLAB * SLAB_ATOMS * 3 // 4, SLAB_ATOMS, 2).astype(jnp.int32),
        "reciprocal_lattice_modes": centred(splits[5], (3, RECIP_MODES), 1.0, 4.0, ((1, 8),), jnp.float32),
        "edge_update_matrix": centred(splits[6], (LAYERS, C, C), C ** -0.5, 0.5),
        "node_update_matrix": centred(splits[7], (LAYERS, C, C), C ** -0.5, 0.5),
        "distance_basis_mixing": centred(splits[8], (LAYERS, NB, C), NB ** -0.5, 2.0, (), jnp.float32),
        "latent_ionic_readout": centred(splits[9], (C, LATENT), C ** -0.5, 0.5),
    }


def bessel_basis(offsets, box_length, count):
    wrapped = jnp.where(offsets[0] > 0.5 * box_length, offsets[0] - box_length, offsets[0])
    wrapped = jnp.where(wrapped < -0.5 * box_length, wrapped + box_length, wrapped)
    distance = jnp.sqrt(wrapped * wrapped + offsets[1] * offsets[1] + offsets[2] * offsets[2] + 0.04)
    orders = jnp.arange(1, count + 1).astype(jnp.float32).reshape((count,) + (1,) * distance.ndim)
    return math.sqrt(2.0 / 3.0) * jnp.sin(orders * (math.pi / 3.0) * distance) / distance

def interact(hidden, gathered_rows, basis, usable, rad_weight, self_weight):
    radial = jnp.einsum('bae,bc->aec', basis, rad_weight, precision=lax.Precision.HIGHEST)
    terms = radial * gathered_rows.astype(jnp.float32)
    summed = lax.optimization_barrier(jnp.sum(jnp.where(usable[:, :, None], terms, 0.0), axis=1)) * 0.125
    self_term = jnp.dot(hidden, self_weight, preferred_element_type=jnp.float32)
    return (hidden.astype(jnp.float32) + jax.nn.silu(summed + self_term)).astype(jnp.bfloat16)

def reference(atom_descriptors, atom_locations, adjacent_atom_slots, neighbour_tally, filled_slot_tallies, reciprocal_lattice_modes, edge_update_matrix, node_update_matrix, distance_basis_mixing, latent_ionic_readout):
    box_length = float(N_SLAB)
    row_ids = jnp.arange(ATOMS, dtype=jnp.int32)
    local_rows = row_ids % SLAB_ATOMS
    slab_of = row_ids // SLAB_ATOMS
    occupied = local_rows < filled_slot_tallies[slab_of]
    global_rows = (slab_of[:, None] + adjacent_atom_slots // SLAB_ATOMS - 1) % N_SLAB * SLAB_ATOMS + adjacent_atom_slots % SLAB_ATOMS
    global_rows = global_rows.astype(jnp.int32)
    slot_ids = jnp.arange(NEIGH, dtype=jnp.int32)
    usable = (slot_ids[None, :] < neighbour_tally[:, None]) & occupied[global_rows] & occupied[:, None]
    offsets = atom_locations[:, global_rows] - atom_locations[:, :, None]
    basis = bessel_basis(offsets, box_length, NB)
    basis_blocks = jnp.transpose(basis.reshape(NB, N_SLAB, SLAB_ATOMS, NEIGH), (1, 0, 2, 3))
    rows_blocks = global_rows.reshape(N_SLAB, SLAB_ATOMS, NEIGH)
    usable_blocks = usable.reshape(N_SLAB, SLAB_ATOMS, NEIGH)
    hidden = atom_descriptors
    for layer_idx in range(LAYERS):
        message_rows = jnp.dot(hidden, edge_update_matrix[layer_idx], preferred_element_type=jnp.float32).astype(jnp.bfloat16)

        def per_slab(blocks):
            hidden_block, rows_block, basis_block, usable_block = blocks
            return interact(hidden_block, message_rows[rows_block], basis_block, usable_block, distance_basis_mixing[layer_idx], node_update_matrix[layer_idx])
        hidden = lax.map(per_slab, (hidden.reshape(N_SLAB, SLAB_ATOMS, C), rows_blocks, basis_blocks, usable_blocks)).reshape(ATOMS, C)
    charges = jnp.dot(hidden, latent_ionic_readout, preferred_element_type=jnp.float32) * occupied[:, None].astype(jnp.float32)
    mode_norm_square = lax.optimization_barrier(jnp.sum(reciprocal_lattice_modes * reciprocal_lattice_modes, axis=0))
    mode_ewald_coefficient = 4.0 * jnp.exp(-mode_norm_square / 8.0) / ((mode_norm_square + 1.0) * math.sqrt(ATOMS * RECIP_MODES))
    mode_batch_index = min(RECIP_MODES, 512)
    mode_batch_number_all = jnp.transpose(reciprocal_lattice_modes.reshape(3, RECIP_MODES // mode_batch_index, mode_batch_index), (1, 0, 2))
    weight_blocks = mode_ewald_coefficient.reshape(RECIP_MODES // mode_batch_index, mode_batch_index)
    coords = atom_locations.T

    def structure(kblk):
        structure_arguments = jnp.dot(coords, kblk, precision=lax.Precision.HIGHEST, preferred_element_type=jnp.float32)
        real_component = jnp.dot(jnp.cos(structure_arguments).T, charges, precision=lax.Precision.HIGHEST, preferred_element_type=jnp.float32)
        imaginary_component = jnp.dot(jnp.sin(structure_arguments).T, charges, precision=lax.Precision.HIGHEST, preferred_element_type=jnp.float32)
        return (real_component, imaginary_component)
    real_all, imag_all = lax.map(structure, mode_batch_number_all)

    def respond(carry, blocks):
        potential_acc, forces_acc = carry
        kblk, wblk, real_component, imaginary_component = blocks
        structure_arguments = jnp.dot(coords, kblk, precision=lax.Precision.HIGHEST, preferred_element_type=jnp.float32)
        cosine_terms = jnp.cos(structure_arguments)
        sine_terms = jnp.sin(structure_arguments)
        weighted_real = wblk[:, None] * real_component
        weighted_imag = wblk[:, None] * imaginary_component
        potential_acc = potential_acc + jnp.dot(cosine_terms, weighted_real, precision=lax.Precision.HIGHEST, preferred_element_type=jnp.float32) + jnp.dot(sine_terms, weighted_imag, precision=lax.Precision.HIGHEST, preferred_element_type=jnp.float32)
        real_drive = jnp.dot(charges, weighted_real.T, precision=lax.Precision.HIGHEST, preferred_element_type=jnp.float32)
        imag_drive = jnp.dot(charges, weighted_imag.T, precision=lax.Precision.HIGHEST, preferred_element_type=jnp.float32)
        gradient_k = imag_drive * cosine_terms - real_drive * sine_terms
        forces_acc = forces_acc - jnp.dot(gradient_k, kblk.T, precision=lax.Precision.HIGHEST, preferred_element_type=jnp.float32)
        return ((potential_acc, forces_acc), None)
    start = (jnp.zeros((ATOMS, LATENT), jnp.float32), jnp.zeros((ATOMS, 3), jnp.float32))
    (potential, forces), _ = lax.scan(respond, start, (mode_batch_number_all, weight_blocks, real_all, imag_all))
    return (potential.T, forces.T)
```

```python
import math

import jax
import jax.numpy as jnp
from jax import lax
from jax.experimental import pallas as pl
from jax.experimental.pallas import tpu as pltpu
from jax.sharding import PartitionSpec as P

AXES = ("slab", "kgrp")
F32 = jnp.float32
BF16 = jnp.bfloat16
MIB = 1 << 20

ROWS = 128
PAYLOAD = 144

CENTRE = 3.04
SINC = (4.53143365e-01, -1.10011030e-01, 6.70800349e-03, -1.85302418e-04, 2.92602795e-06, -2.98676509e-08)
TWOCOS = (-5.04597246e-01, -5.81178942e-01, 7.05473141e-02, -2.86778430e-03, 5.94149034e-05, -7.50432042e-07, 6.38391477e-09)
SINTURN = (6.2831853, -41.34170041, 81.60513139, -76.70301535, 42.02592698, -14.89984666, 3.2381375)
COSTURN = (0.99999999, -19.7392045, 64.93911746, -85.45013953, 60.16763095, -25.96759925, 6.52865816)


def horner(coefficients, x):
    value = coefficients[-1] * x + coefficients[-2]
    for c in coefficients[-3::-1]:
        value = value * x + c
    return value


def split(x, parts):
    pieces = []
    for i in range(parts):
        piece = x.astype(BF16)
        pieces.append(piece)
        if i + 1 < parts:
            x = x - piece.astype(F32)
    return pieces


def nt(a, b):
    return lax.dot_general(a, b, (((1,), (1,)), ((), ())), preferred_element_type=F32)


def nn(a, b):
    return jnp.dot(a, b, preferred_element_type=F32)


def call(body, out_shape, *operands, scalars=(), name, flops=0, limit=32, **kw):
    specs = [pl.BlockSpec(memory_space=pltpu.SMEM)] * len(scalars)
    in_specs = specs + kw.pop("in_specs", [pl.BlockSpec(memory_space=pltpu.VMEM)] * len(operands))
    return pl.pallas_call(
        body,
        out_shape=out_shape,
        in_specs=in_specs,
        name=name,
        cost_estimate=pl.CostEstimate(flops=flops, bytes_accessed=MIB, transcendentals=0),
        compiler_params=pltpu.CompilerParams(vmem_limit_bytes=limit * MIB),
        **kw,
    )(*scalars, *operands)


def pack_body(desc_ref, loc_ref, out_ref):
    out_ref[0:ROWS, :] = desc_ref[...]
    hi, mid, lo = [p.astype(F32) for p in split(loc_ref[...], 3)]
    tail = jnp.concatenate([hi, mid, lo, jnp.zeros((7, ROWS), F32)], axis=0)
    out_ref[ROWS:PAYLOAD, :] = tail.astype(BF16)


def coordinates(payload):
    tail = payload[ROWS:PAYLOAD, :].astype(F32)
    return (tail[0:3] + tail[3:6]) + tail[6:9]


def count_body(scal_ref, slots_ref, tally_ref, cnt_ref):
    y, zh, odd = scal_ref[0], scal_ref[1], scal_ref[2]
    f_prev, f_own, f_next, base = scal_ref[3], scal_ref[4], scal_ref[5], scal_ref[6]
    slots = slots_ref[...]
    shape = slots.shape
    lane = lax.broadcasted_iota(jnp.int32, shape, 1)
    row = lax.broadcasted_iota(jnp.int32, shape, 0)
    local = lane >> 6
    atom = row * 8 + local + base
    region = slots >> 10
    within = slots & 1023
    filled = jnp.where(region == 0, f_prev, jnp.where(region == 1, f_own, f_next))
    usable = ((lane & 63) < tally_ref[...]) & (within < filled) & (atom < f_own)
    place = jnp.where(region == 1, 0, jnp.where(region == 2 * odd, 1, 2))
    kblock = within >> 7
    inner = ((((kblock >> 1) - y) & 3) << 1) | ((kblock & 1) ^ zh)
    target = jnp.where(usable, (place * 8 + inner) * 8 + local, -1)
    low = slots & 127
    iota_p = lax.broadcasted_iota(jnp.int32, (192, 512), 0)
    iota_l = lax.broadcasted_iota(jnp.int32, (128, 512), 0)
    for i in range(16):
        p = jnp.where(iota_p == target[i : i + 1], 1.0, 0.0).astype(BF16)
        l = jnp.where(iota_l == low[i : i + 1], 1.0, 0.0).astype(BF16)
        cnt_ref[:, 8 * i : 8 * i + 8, :] = nt(p, l).reshape(24, 8, 128)


def update(gathered, hidden, self_weight):
    drive = gathered * 0.125 + nn(hidden, self_weight)
    return (hidden.astype(F32) + drive * jax.nn.sigmoid(drive)).astype(BF16)


def mix(acc, mixing):
    total = acc[0:ROWS] * mixing[0:1]
    for n in range(1, 8):
        total = total + acc[n * ROWS : (n + 1) * ROWS] * mixing[n : n + 1]
    return total


def first_body(shift_ref, y0, y1, y2, y3, c0, c1, c2, c3, cnt_ref, here_ref, edge_ref, node_ref, mixing_ref, g_ref, hidden_ref, message_ref, m_s, x_s, acc_s):
    step = pl.program_id(0)

    @pl.when(step == 0)
    def _():
        for b in range(24):
            j, z = (b % 8) // 2, b % 2
            ref = (y0, y1, y2, y3)[j] if b < 16 else (c0, c1, c2, c3)[j]
            i = (b // 8) * 2 + z if b < 16 else z
            m_s[b // 4, (b % 4) * ROWS : (b % 4 + 1) * ROWS, :] = nn(ref[i, 0:ROWS, :], edge_ref[0]).astype(BF16)
            xyz = coordinates(ref[i])
            x_s[b, 0:1, :] = xyz[0:1] + shift_ref[b // 8]
            x_s[b, 1:3, :] = xyz[1:3]
        acc_s[...] = jnp.zeros_like(acc_s)

    for q in range(4):
        src = x_s[step * 4 + q]
        for r in range(0, ROWS, 64):
            here = here_ref[r : r + 64, :]
            dx = src[0:1] - here[:, 0:1]
            dy = src[1:2] - here[:, 1:2]
            dz = src[2:3] - here[:, 2:3]
            v = dx * dx + dy * dy + dz * dz + (0.04 - CENTRE)
            cur = cnt_ref[q, r : r + 64, :] * horner(SINC, v)
            turn = horner(TWOCOS, v)
            prev = None
            for n in range(8):
                g_ref[n * ROWS + r : n * ROWS + r + 64, q * 128 : (q + 1) * 128] = cur.astype(BF16)
                nxt = turn * cur if prev is None else turn * cur - prev
                prev, cur = cur, nxt
    acc_s[...] += nn(g_ref[...], m_s[step])

    @pl.when(step == 5)
    def _():
        hidden = update(mix(acc_s[...], mixing_ref[0]), y0[0, 0:ROWS, :], node_ref[0])
        hidden_ref[...] = hidden
        message_ref[...] = nn(hidden, edge_ref[1]).astype(BF16)


def second_body(scal_ref, y0, y1, y2, y3, c0, c1, c2, c3, g_ref, hidden_ref, node_ref, mixing_ref, readout_ref, charge_ref, m_s, acc_s):
    step = pl.program_id(0)

    @pl.when(step == 0)
    def _():
        for b in range(24):
            j, z = (b % 8) // 2, b % 2
            ref = (y0, y1, y2, y3)[j] if b < 16 else (c0, c1, c2, c3)[j]
            i = (b // 8) * 2 + z if b < 16 else z
            m_s[b // 4, (b % 4) * ROWS : (b % 4 + 1) * ROWS, :] = ref[i]
        acc_s[...] = jnp.zeros_like(acc_s)

    acc_s[...] += nn(g_ref[...], m_s[step])

    @pl.when(step == 5)
    def _():
        hidden = update(mix(acc_s[...], mixing_ref[1]), hidden_ref[...], node_ref[1])
        charges = nt(readout_ref[...], hidden)
        atom = lax.broadcasted_iota(jnp.int32, charges.shape, 1) + scal_ref[6]
        charge_ref[...] = jnp.where(atom < scal_ref[4], charges, 0.0)


def phase_body(y0, y1, y2, y3, modes_ref, wave_ref):
    for b in range(8):
        xyz = coordinates((y0, y1, y2, y3)[b // 2][b % 2])
        for r in range(0, 1024, 64):
            k = modes_ref[r : r + 64, :]
            turns = k[:, 0:1] * xyz[0:1] + k[:, 1:2] * xyz[1:2] + k[:, 2:3] * xyz[2:3]
            rest = turns - jnp.round(turns)
            square = rest * rest
            wave_ref[r : r + 64, b * 128 : (b + 1) * 128] = horner(COSTURN, square).astype(BF16)
            wave_ref[1024 + r : 1024 + r + 64, b * 128 : (b + 1) * 128] = (rest * horner(SINTURN, square)).astype(BF16)


def structure_body(place_ref, wave_ref, charge_ref, out_ref, q_ref):
    charges = jnp.concatenate([charge_ref[place_ref[b]] for b in range(8)], axis=1)
    q_ref[...] = charges
    pieces = jnp.concatenate(split(charges, 3), axis=0)
    for i in range(2):
        for r in range(0, 1024, 128):
            s = nt(wave_ref[i * 1024 + r : i * 1024 + r + 128, :], pieces)
            s = s[:, 0:16] + s[:, 16:32] + s[:, 32:48]
            out_ref[i * 16 : (i + 1) * 16, r : r + 128] = s.T


def respond_body(place_ref, scale_ref, wave_ref, sum_ref, q_ref, modes_ref, out_ref):
    k = modes_ref[...]
    square = k[0:1] * k[0:1] + k[1:2] * k[1:2] + k[2:3] * k[2:3]
    weight = scale_ref[0] * jnp.exp(square * -0.125) / (square + 1.0)
    real = sum_ref[0:16, :] * weight
    imag = sum_ref[16:32, :] * weight
    left = [real] + [imag * k[j : j + 1] for j in range(3)]
    right = [imag] + [real * -k[j : j + 1] for j in range(3)]
    both = jnp.concatenate([jnp.concatenate(left, axis=0), jnp.concatenate(right, axis=0)], axis=1)
    out = nn(jnp.concatenate(split(both, 2), axis=0), wave_ref[...])
    out = out[0:64] + out[64:128]
    force = [-jnp.sum(out[16 * j + 16 : 16 * j + 32] * q_ref[...], axis=0, keepdims=True) for j in range(3)]
    full = jnp.concatenate([out[0:16]] + force + [jnp.zeros((5, 1024), F32)], axis=0)
    for b in range(8):
        out_ref[place_ref[b]] = full[:, b * 128 : (b + 1) * 128]


def pairs(n_slab, target):
    return [(s * 8 + k, (target(s, k)[0] % n_slab) * 8 + target(s, k)[1]) for s in range(n_slab) for k in range(8)]


def move(x, target):
    return lax.ppermute(x, AXES, pairs(lax.axis_size("slab"), target))


def over_chip(s):
    return s + 1 if s % 2 else s - 1


def surroundings(block):
    near = move(block, lambda s, k: (over_chip(s), k))
    half = move(block, lambda s, k: (s, k ^ 1))
    both = move(block, lambda s, k: (over_chip(s), k ^ 1))
    stack = jnp.stack([block, half, near, both])
    ys = [stack]
    for j in range(1, 4):
        ys.append(move(stack, lambda s, k: (s, (k - 2 * j) % 8)))
    cs = [move(y[0:2], lambda s, k: (s ^ 1, k)) for y in ys]
    return ys + cs


def shards(
    atom_descriptors,
    atom_locations,
    adjacent_atom_slots,
    neighbour_tally,
    filled_slot_tallies,
    reciprocal_lattice_modes,
    edge_update_matrix,
    node_update_matrix,
    distance_basis_mixing,
    latent_ionic_readout,
):
    n_slab = lax.axis_size("slab")
    slab = lax.axis_index("slab")
    group = lax.axis_index("kgrp")
    odd = slab % 2
    y, zh = group // 2, group % 2
    filled = jnp.take(filled_slot_tallies, (slab + jnp.arange(3) - 1) % n_slab)
    scal = jnp.concatenate([jnp.stack([y, zh, odd]), filled, jnp.stack([group * ROWS, 0])]).astype(jnp.int32)
    low_edge = jnp.where(slab == 0, -float(n_slab), 0.0)
    high_edge = jnp.where(slab == n_slab - 1, float(n_slab), 0.0)
    shift = jnp.stack([0.0, jnp.where(odd == 1, high_edge, low_edge), jnp.where(odd == 1, low_edge, high_edge)]).astype(F32)
    spots = jnp.arange(8, dtype=jnp.int32)
    place = (((y + spots // 2) % 4) * 2 + ((spots % 2) ^ zh)).astype(jnp.int32)

    block = call(pack_body, jax.ShapeDtypeStruct((PAYLOAD, ROWS), BF16), atom_descriptors, atom_locations, name="pack")
    first = surroundings(block)
    counts = call(
        count_body,
        jax.ShapeDtypeStruct((24, ROWS, 128), F32),
        adjacent_atom_slots.reshape(16, 512),
        jnp.broadcast_to(neighbour_tally[:, None], (ROWS, 64)).reshape(16, 512),
        scalars=(scal,),
        name="counts",
        flops=10**9,
    )
    whole = lambda *shape: pl.BlockSpec(shape, lambda i: (0,) * len(shape))
    near_specs = lambda rows: [whole(4, rows, ROWS)] * 4 + [whole(2, rows, ROWS)] * 4
    basis, hidden, messages = call(
        first_body,
        (
            jax.ShapeDtypeStruct((8 * ROWS, 24 * ROWS), BF16),
            jax.ShapeDtypeStruct((ROWS, 128), BF16),
            jax.ShapeDtypeStruct((ROWS, 128), BF16),
        ),
        *first,
        counts,
        atom_locations.T,
        edge_update_matrix,
        node_update_matrix,
        distance_basis_mixing,
        scalars=(shift,),
        name="first_layer",
        flops=10**9,
        grid=(6,),
        in_specs=near_specs(PAYLOAD)
        + [pl.BlockSpec((4, ROWS, 128), lambda i: (i, 0, 0)), whole(ROWS, 3), whole(2, 128, 128), whole(2, 128, 128), whole(2, 8, 128)],
        out_specs=[pl.BlockSpec((8 * ROWS, 512), lambda i: (0, i)), whole(ROWS, 128), whole(ROWS, 128)],
        scratch_shapes=[pltpu.VMEM((6, 512, 128), BF16), pltpu.VMEM((24, 3, 128), F32), pltpu.VMEM((8 * ROWS, 128), F32)],
    )
    second = surroundings(messages)
    turns = reciprocal_lattice_modes.T * (0.5 / math.pi)
    waves = call(
        phase_body, jax.ShapeDtypeStruct((2048, 1024), BF16), *first[:4], turns, name="phases", flops=2 * 10**9
    )
    charges = call(
        second_body,
        jax.ShapeDtypeStruct((16, ROWS), F32),
        *second,
        basis,
        hidden,
        node_update_matrix,
        distance_basis_mixing,
        latent_ionic_readout.T,
        scalars=(scal,),
        name="second_layer",
        flops=10**9,
        grid=(6,),
        in_specs=near_specs(ROWS)
        + [pl.BlockSpec((8 * ROWS, 512), lambda i: (0, i)), whole(ROWS, 128), whole(2, 128, 128), whole(2, 8, 128), whole(16, 128)],
        out_specs=whole(16, ROWS),
        scratch_shapes=[pltpu.VMEM((6, 512, 128), BF16), pltpu.VMEM((8 * ROWS, 128), F32)],
    )
    slab_charges = lax.all_to_all(jnp.broadcast_to(charges[None], (8, 16, ROWS)), "kgrp", 0, 0)
    sums, q = call(
        structure_body,
        (jax.ShapeDtypeStruct((32, 1024), F32), jax.ShapeDtypeStruct((16, 1024), F32)),
        waves,
        slab_charges,
        scalars=(place,),
        name="structure",
        flops=10**8,
    )
    lower, upper = sums[:, :512], sums[:, 512:]
    is_odd = odd == 1
    part = jnp.where(is_odd, upper, lower) + move(jnp.where(is_odd, lower, upper), lambda s, k: (s ^ 1, k))
    part = part + sum(move(part, lambda s, k, m=m: (s ^ (2 * m), k)) for m in (1, 2, 3))
    part = part + sum(move(part, lambda s, k, m=m: (s + 8 * m, k)) for m in (1, 2, 3))
    other = move(part, lambda s, k: (s ^ 1, k))
    total = jnp.where(is_odd, jnp.concatenate([other, part], axis=1), jnp.concatenate([part, other], axis=1))
    scale = jnp.full((1,), 4.0 / math.sqrt(n_slab * 1024 * reciprocal_lattice_modes.shape[1] * 8), F32)
    partial = call(
        respond_body,
        jax.ShapeDtypeStruct((8, 24, ROWS), F32),
        waves,
        total,
        q,
        reciprocal_lattice_modes,
        scalars=(place, scale),
        name="respond",
        flops=10**8,
    )
    result = jnp.sum(lax.all_to_all(partial, "kgrp", 0, 0), axis=0)
    return result[:16], result[16:19]


def solution(mesh):
    return jax.shard_map(
        shards,
        mesh=mesh,
        in_specs=(
            P(("slab", "kgrp"), None),
            P(None, ("slab", "kgrp")),
            P(("slab", "kgrp"), None),
            P(("slab", "kgrp")),
            P(),
            P(None, "kgrp"),
            P(),
            P(),
            P(),
            P(),
        ),
        out_specs=(P(None, ("slab", "kgrp")), P(None, ("slab", "kgrp"))),
        check_vma=False,
    )
```

```python
import math

import jax
import jax.numpy as jnp
from jax import lax
from jax.experimental import pallas as pl
from jax.experimental.pallas import tpu as pltpu
from jax.sharding import PartitionSpec as P

AXES = ("slab", "kgrp")
F32 = jnp.float32
BF16 = jnp.bfloat16
MIB = 1 << 20

ROWS = 128
PAYLOAD = 144

CENTRE = 3.04
SINC = (4.53143365e-01, -1.10011030e-01, 6.70800349e-03, -1.85302418e-04, 2.92602795e-06, -2.98676509e-08)
TWOCOS = (-5.04597246e-01, -5.81178942e-01, 7.05473141e-02, -2.86778430e-03, 5.94149034e-05, -7.50432042e-07, 6.38391477e-09)
SINTURN = (6.2831853, -41.34170041, 81.60513139, -76.70301535, 42.02592698, -14.89984666, 3.2381375)
COSTURN = (0.99999999, -19.7392045, 64.93911746, -85.45013953, 60.16763095, -25.96759925, 6.52865816)


def horner(coefficients, x):
    value = coefficients[-1] * x + coefficients[-2]
    for c in coefficients[-3::-1]:
        value = value * x + c
    return value


def split(x, parts):
    pieces = []
    for i in range(parts):
        piece = x.astype(BF16)
        pieces.append(piece)
        if i + 1 < parts:
            x = x - piece.astype(F32)
    return pieces


def nt(a, b):
    return lax.dot_general(a, b, (((1,), (1,)), ((), ())), preferred_element_type=F32)


def nn(a, b):
    return jnp.dot(a, b, preferred_element_type=F32)


def call(body, out_shape, *operands, scalars=(), after=(), name, flops=0, limit=12, scratch=()):
    n, m = len(scalars) + len(operands), len(after)
    return pl.pallas_call(
        lambda *refs: body(*refs[:n], *refs[n + m :]),
        out_shape=out_shape,
        in_specs=[pl.BlockSpec(memory_space=pltpu.SMEM)] * len(scalars)
        + [pl.BlockSpec(memory_space=pltpu.VMEM)] * len(operands)
        + [pl.BlockSpec(memory_space=pl.ANY)] * m,
        scratch_shapes=list(scratch),
        name=name,
        cost_estimate=pl.CostEstimate(flops=flops, bytes_accessed=MIB, transcendentals=0),
        compiler_params=pltpu.CompilerParams(vmem_limit_bytes=limit * MIB),
    )(*scalars, *operands, *after)


def pack_body(desc_ref, loc_ref, out_ref):
    out_ref[0:ROWS, :] = desc_ref[...]
    hi, mid, lo = [p.astype(F32) for p in split(loc_ref[...], 3)]
    tail = jnp.concatenate([hi, mid, lo, jnp.zeros((7, ROWS), F32)], axis=0)
    out_ref[ROWS:PAYLOAD, :] = tail.astype(BF16)


def coordinates(payload):
    tail = payload[ROWS:PAYLOAD, :].astype(F32)
    return (tail[0:3] + tail[3:6]) + tail[6:9]


def count_body(scal_ref, slots_ref, tally_ref, *cnt_refs):
    y, zh, odd = scal_ref[0], scal_ref[1], scal_ref[2]
    f_prev, f_own, f_next, base = scal_ref[3], scal_ref[4], scal_ref[5], scal_ref[6]
    slots = slots_ref[...]
    shape = slots.shape
    lane = lax.broadcasted_iota(jnp.int32, shape, 1)
    row = lax.broadcasted_iota(jnp.int32, shape, 0)
    local = lane >> 6
    atom = row * 8 + local + base
    region = slots >> 10
    within = slots & 1023
    filled = jnp.where(region == 0, f_prev, jnp.where(region == 1, f_own, f_next))
    usable = ((lane & 63) < tally_ref[...]) & (within < filled) & (atom < f_own)
    kblock = within >> 7
    place = jnp.where(region == 1, 0, jnp.where(region == 2 * odd, 2, 4)) + ((kblock & 1) ^ zh)
    target = jnp.where(usable, ((((kblock >> 1) - y) & 3) * 6 + place) * 8 + local, -1)
    low = slots & 127
    iota_p = lax.broadcasted_iota(jnp.int32, (192, 512), 0)
    iota_l = lax.broadcasted_iota(jnp.int32, (128, 512), 0)
    for i in range(16):
        p = jnp.where(iota_p == target[i : i + 1], 1.0, 0.0).astype(BF16)
        l = jnp.where(iota_l == low[i : i + 1], 1.0, 0.0).astype(BF16)
        c = nt(p, l).reshape(24, 8, 128)
        for j in range(4):
            cnt_refs[j][:, 8 * i : 8 * i + 8, :] = c[6 * j : 6 * j + 6]


def update(gathered, hidden, self_weight):
    drive = gathered * 0.125 + nn(hidden, self_weight)
    return (hidden.astype(F32) + drive * jax.nn.sigmoid(drive)).astype(BF16)


def mix(acc, mixing):
    total = acc[0:ROWS] * mixing[0:1]
    for n in range(1, 8):
        total = total + acc[n * ROWS : (n + 1) * ROWS] * mixing[n : n + 1]
    return total


def block_of(y_ref, c_ref, i):
    return y_ref[i] if i < 4 else c_ref[i - 4]


def basis_part(shift_ref, y_ref, c_ref, cnt_ref, here_ref, edge_ref, mixing_ref, g_ref):
    rows = []
    for i in range(6):
        payload = block_of(y_ref, c_ref, i)
        rows.append(nn(payload[0:ROWS, :], edge_ref[0]).astype(BF16))
        xyz = coordinates(payload)
        x = xyz[0:1] + shift_ref[i // 2]
        for r in range(0, ROWS, 64):
            here = here_ref[r : r + 64, :]
            dx = x - here[:, 0:1]
            dy = xyz[1:2] - here[:, 1:2]
            dz = xyz[2:3] - here[:, 2:3]
            v = dx * dx + dy * dy + dz * dz + (0.04 - CENTRE)
            cur = cnt_ref[i, r : r + 64, :] * horner(SINC, v)
            turn = horner(TWOCOS, v)
            prev = None
            for n in range(8):
                g_ref[n * ROWS + r : n * ROWS + r + 64, i * 128 : (i + 1) * 128] = cur.astype(BF16)
                nxt = turn * cur if prev is None else turn * cur - prev
                prev, cur = cur, nxt
    return mix(nn(g_ref[...], jnp.concatenate(rows, axis=0)), mixing_ref[0])


def first_body(shift_ref, y_ref, c_ref, cnt_ref, here_ref, edge_ref, mixing_ref, g_ref, part_ref):
    part_ref[...] = basis_part(shift_ref, y_ref, c_ref, cnt_ref, here_ref, edge_ref, mixing_ref, g_ref)


def first_last_body(shift_ref, y_ref, c_ref, cnt_ref, here_ref, edge_ref, mixing_ref, p0, p1, p2, own_ref, node_ref, g_ref, hidden_ref, message_ref):
    gathered = basis_part(shift_ref, y_ref, c_ref, cnt_ref, here_ref, edge_ref, mixing_ref, g_ref)
    gathered = ((p0[...] + p1[...]) + p2[...]) + gathered
    hidden = update(gathered, own_ref[0, 0:ROWS, :], node_ref[0])
    hidden_ref[...] = hidden
    message_ref[...] = nn(hidden, edge_ref[1]).astype(BF16)


def gather_part(y_ref, c_ref, g_ref):
    return nn(g_ref[...], jnp.concatenate([block_of(y_ref, c_ref, i) for i in range(6)], axis=0))


def second_body(y_ref, c_ref, g_ref, mixing_ref, part_ref):
    part_ref[...] = mix(gather_part(y_ref, c_ref, g_ref), mixing_ref[1])


def second_last_body(scal_ref, y_ref, c_ref, g_ref, mixing_ref, p0, p1, p2, hidden_ref, node_ref, readout_ref, charge_ref):
    gathered = ((p0[...] + p1[...]) + p2[...]) + mix(gather_part(y_ref, c_ref, g_ref), mixing_ref[1])
    hidden = update(gathered, hidden_ref[...], node_ref[1])
    charges = nt(readout_ref[...], hidden)
    atom = lax.broadcasted_iota(jnp.int32, charges.shape, 1) + scal_ref[6]
    charges = jnp.where(atom < scal_ref[4], charges, 0.0)
    for i in range(8):
        charge_ref[i] = charges


def stack_body(a, b, c, d, out_ref):
    for i, ref in enumerate((a, b, c, d)):
        out_ref[i] = ref[...]


def phase_body(y_ref, modes_ref, wave_ref):
    for b in range(2):
        xyz = coordinates(y_ref[b])
        for r in range(0, 1024, 64):
            k = modes_ref[r : r + 64, :]
            turns = k[:, 0:1] * xyz[0:1] + k[:, 1:2] * xyz[1:2] + k[:, 2:3] * xyz[2:3]
            rest = turns - jnp.round(turns)
            square = rest * rest
            wave_ref[r : r + 64, b * 128 : (b + 1) * 128] = horner(COSTURN, square).astype(BF16)
            wave_ref[1024 + r : 1024 + r + 64, b * 128 : (b + 1) * 128] = (rest * horner(SINTURN, square)).astype(BF16)


def structure_body(place_ref, w0, w1, w2, w3, charge_ref, out_ref, q_ref):
    charges = jnp.concatenate([charge_ref[place_ref[b]] for b in range(8)], axis=1)
    q_ref[...] = charges
    pieces = jnp.concatenate(split(charges, 3), axis=0)
    for i in range(2):
        for r in range(i * 1024, (i + 1) * 1024, 256):
            s = nt(w0[r : r + 256, :], pieces[:, 0:256])
            for j, w in enumerate((w1, w2, w3), 1):
                s = s + nt(w[r : r + 256, :], pieces[:, j * 256 : (j + 1) * 256])
            s = s[:, 0:16] + s[:, 16:32] + s[:, 32:48]
            out_ref[i * 16 : (i + 1) * 16, r - i * 1024 : r - i * 1024 + 256] = s.T


def respond_body(place_ref, scale_ref, w0, w1, w2, w3, sum_ref, q_ref, modes_ref, out_ref):
    k = modes_ref[...]
    square = k[0:1] * k[0:1] + k[1:2] * k[1:2] + k[2:3] * k[2:3]
    weight = scale_ref[0] * jnp.exp(square * -0.125) / (square + 1.0)
    real = sum_ref[0:16, :] * weight
    imag = sum_ref[16:32, :] * weight
    left = [real] + [imag * k[j : j + 1] for j in range(3)]
    right = [imag] + [real * -k[j : j + 1] for j in range(3)]
    both = jnp.concatenate([jnp.concatenate(left, axis=0), jnp.concatenate(right, axis=0)], axis=1)
    pieces = jnp.concatenate(split(both, 2), axis=0)
    for i, w in enumerate((w0, w1, w2, w3)):
        out = nn(pieces, w[...])
        out = out[0:64] + out[64:128]
        q = q_ref[:, i * 256 : (i + 1) * 256]
        force = [-jnp.sum(out[16 * j + 16 : 16 * j + 32] * q, axis=0, keepdims=True) for j in range(3)]
        full = jnp.concatenate([out[0:16]] + force + [jnp.zeros((5, 256), F32)], axis=0)
        for b in range(2):
            out_ref[place_ref[2 * i + b]] = full[:, b * 128 : (b + 1) * 128]


def finish_body(parts_ref, potential_ref, forces_ref):
    total = parts_ref[0]
    for i in range(1, 8):
        total = total + parts_ref[i]
    potential_ref[...] = total[0:16]
    forces_ref[...] = total[16:19]


def pairs(n_slab, target):
    return [(s * 8 + k, (target(s, k)[0] % n_slab) * 8 + target(s, k)[1]) for s in range(n_slab) for k in range(8)]


def move(x, target):
    return lax.ppermute(x, AXES, pairs(lax.axis_size("slab"), target))


def over_chip(s):
    return s + 1 if s % 2 else s - 1


def near_blocks(block):
    half = move(block, lambda s, k: (s, k ^ 1))
    near = move(block, lambda s, k: (over_chip(s), k))
    both = move(block, lambda s, k: (over_chip(s), k ^ 1))
    return half, near, both


def surroundings(block, near, name, after):
    stack = call(stack_body, jax.ShapeDtypeStruct((4,) + block.shape, BF16), block, *near, name=name, after=after)
    ys = [stack]
    for j in range(1, 4):
        ys.append(move(stack, lambda s, k: (s, (k - 2 * j) % 8)))
    return ys, [move(y[0:2], lambda s, k: (s ^ 1, k)) for y in ys]


def shards(
    atom_descriptors,
    atom_locations,
    adjacent_atom_slots,
    neighbour_tally,
    filled_slot_tallies,
    reciprocal_lattice_modes,
    edge_update_matrix,
    node_update_matrix,
    distance_basis_mixing,
    latent_ionic_readout,
):
    n_slab = lax.axis_size("slab")
    slab = lax.axis_index("slab")
    group = lax.axis_index("kgrp")
    odd = slab % 2
    y, zh = group // 2, group % 2
    filled = jnp.take(filled_slot_tallies, (slab + jnp.arange(3) - 1) % n_slab)
    scal = jnp.concatenate([jnp.stack([y, zh, odd]), filled, jnp.stack([group * ROWS, 0])]).astype(jnp.int32)
    low_edge = jnp.where(slab == 0, -float(n_slab), 0.0)
    high_edge = jnp.where(slab == n_slab - 1, float(n_slab), 0.0)
    shift = jnp.stack([0.0, jnp.where(odd == 1, high_edge, low_edge), jnp.where(odd == 1, low_edge, high_edge)]).astype(F32)
    spots = jnp.arange(8, dtype=jnp.int32)
    place = (((y + spots // 2) % 4) * 2 + ((spots % 2) ^ zh)).astype(jnp.int32)

    shape = jax.ShapeDtypeStruct
    block = call(pack_body, shape((PAYLOAD, ROWS), BF16), atom_descriptors, atom_locations, name="pack")
    near = near_blocks(block)
    counts = call(
        count_body,
        [shape((6, ROWS, 128), F32)] * 4,
        adjacent_atom_slots.reshape(16, 512),
        jnp.broadcast_to(neighbour_tally[:, None], (ROWS, 64)).reshape(16, 512),
        scalars=(scal,),
        name="counts",
        flops=10**9,
    )
    ys, cs = surroundings(block, near, "stack_first", (counts[0],))
    here = atom_locations.T
    basis, parts = [None] * 4, [None] * 3
    for j in range(3):
        basis[j], parts[j] = call(
            first_body,
            (shape((8 * ROWS, 6 * ROWS), BF16), shape((ROWS, 128), F32)),
            ys[j], cs[j], counts[j], here, edge_update_matrix, distance_basis_mixing,
            scalars=(shift,),
            name=f"first_{j}",
            flops=10**9,
        )
    basis[3], hidden, messages = call(
        first_last_body,
        (shape((8 * ROWS, 6 * ROWS), BF16), shape((ROWS, 128), BF16), shape((ROWS, 128), BF16)),
        ys[3], cs[3], counts[3], here, edge_update_matrix, distance_basis_mixing, *parts, ys[0], node_update_matrix,
        scalars=(shift,),
        name="first_3",
        flops=10**9,
    )
    turns = reciprocal_lattice_modes.T * (0.5 / math.pi)

    def phases(j, after):
        return call(phase_body, shape((2048, 256), BF16), ys[j], turns, name=f"phases_{j}", flops=10**9, after=after)

    near = near_blocks(messages)
    waves = [phases(0, (messages,)), phases(1, (messages,))]
    ms, ns = surroundings(messages, near, "stack_second", waves)
    waves += [phases(2, (ms[0],)), phases(3, (ms[0],))]
    parts = [
        call(
            second_body,
            shape((ROWS, 128), F32),
            ms[j], ns[j], basis[j], distance_basis_mixing,
            name=f"second_{j}",
            flops=10**9,
            after=waves[2:] if j == 0 else (),
        )
        for j in range(3)
    ]
    charges = call(
        second_last_body,
        shape((8, 16, ROWS), F32),
        ms[3], ns[3], basis[3], distance_basis_mixing, *parts, hidden, node_update_matrix, latent_ionic_readout.T,
        scalars=(scal,),
        name="second_3",
        flops=10**9,
    )
    slab_charges = lax.all_to_all(charges, "kgrp", 0, 0)
    sums, q = call(
        structure_body,
        (shape((32, 1024), F32), shape((16, 1024), F32)),
        *waves,
        slab_charges,
        scalars=(place,),
        name="structure",
        flops=10**8,
    )
    lower, upper = sums[:, :512], sums[:, 512:]
    is_odd = odd == 1
    part = jnp.where(is_odd, upper, lower) + move(jnp.where(is_odd, lower, upper), lambda s, k: (s ^ 1, k))
    part = part + sum(move(part, lambda s, k, m=m: (s ^ (2 * m), k)) for m in (1, 2, 3))
    part = part + sum(move(part, lambda s, k, m=m: (s + 8 * m, k)) for m in (1, 2, 3))
    other = move(part, lambda s, k: (s ^ 1, k))
    total = jnp.where(is_odd, jnp.concatenate([other, part], axis=1), jnp.concatenate([part, other], axis=1))
    scale = jnp.full((1,), 4.0 / math.sqrt(n_slab * 1024 * reciprocal_lattice_modes.shape[1] * 8), F32)
    partial = call(
        respond_body,
        shape((8, 24, ROWS), F32),
        *waves,
        total,
        q,
        reciprocal_lattice_modes,
        scalars=(place, scale),
        name="respond",
        flops=10**8,
    )
    partial = lax.all_to_all(partial, "kgrp", 0, 0)
    return tuple(call(finish_body, (shape((16, ROWS), F32), shape((3, ROWS), F32)), partial, name="finish"))


def solution(mesh):
    return jax.shard_map(
        shards,
        mesh=mesh,
        in_specs=(
            P(("slab", "kgrp"), None),
            P(None, ("slab", "kgrp")),
            P(("slab", "kgrp"), None),
            P(("slab", "kgrp")),
            P(),
            P(None, "kgrp"),
            P(),
            P(),
            P(),
            P(),
        ),
        out_specs=(P(None, ("slab", "kgrp")), P(None, ("slab", "kgrp"))),
        check_vma=False,
    )
```

```python
import math

import jax
import jax.numpy as jnp
from jax import lax
from jax.experimental import pallas as pl
from jax.experimental.pallas import tpu as pltpu
from jax.sharding import PartitionSpec as P

AXES = ("slab", "kgrp")
F32 = jnp.float32
BF16 = jnp.bfloat16
MIB = 1 << 20

ROWS = 128
PAYLOAD = 144

CENTRE = 3.04
SINC = (0.4531433647, -0.11001027431, 0.0067080034928, -0.00018563842882, 2.9260279482e-06)
TWOCOS = (-0.504597100576, -0.581178942324, 0.0705470232447, -0.0028677843003, 5.9501086291e-05, -7.504320417652e-07)
SINTURN = (6.283184916495, -41.341589232689, 81.599943329776, -76.614472532619, 41.342882354378, -12.471243534759)
COSTURN = (0.99999921078, -19.738980355764, 64.92865742103, -85.271621534265, 58.790492119989, -21.071105627427)


def horner(coefficients, x):
    value = coefficients[-1] * x + coefficients[-2]
    for c in coefficients[-3::-1]:
        value = value * x + c
    return value


def split(x, parts):
    pieces = []
    for i in range(parts):
        piece = x.astype(BF16)
        pieces.append(piece)
        if i + 1 < parts:
            x = x - piece.astype(F32)
    return pieces


def nt(a, b):
    return lax.dot_general(a, b, (((1,), (1,)), ((), ())), preferred_element_type=F32)


def nn(a, b):
    return jnp.dot(a, b, preferred_element_type=F32)


def call(body, out_shape, *operands, scalars=(), after=(), name, flops=0, limit=12, scratch=()):
    n, m = len(scalars) + len(operands), len(after)
    return pl.pallas_call(
        lambda *refs: body(*refs[:n], *refs[n + m :]),
        out_shape=out_shape,
        in_specs=[pl.BlockSpec(memory_space=pltpu.SMEM)] * len(scalars)
        + [pl.BlockSpec(memory_space=pltpu.VMEM)] * len(operands)
        + [pl.BlockSpec(memory_space=pl.ANY)] * m,
        scratch_shapes=list(scratch),
        name=name,
        cost_estimate=pl.CostEstimate(flops=flops, bytes_accessed=MIB, transcendentals=0),
        compiler_params=pltpu.CompilerParams(vmem_limit_bytes=limit * MIB),
    )(*scalars, *operands, *after)


def pack_body(desc_ref, loc_ref, out_ref):
    out_ref[0:ROWS, :] = desc_ref[...]
    hi, mid, lo = [p.astype(F32) for p in split(loc_ref[...], 3)]
    tail = jnp.concatenate([hi, mid, lo, jnp.zeros((7, ROWS), F32)], axis=0)
    out_ref[ROWS:PAYLOAD, :] = tail.astype(BF16)


def coordinates(payload):
    tail = payload[ROWS:PAYLOAD, :].astype(F32)
    return (tail[0:3] + tail[3:6]) + tail[6:9]


def count_body(scal_ref, slots_ref, *cnt_refs):
    y, zh, odd = scal_ref[0], scal_ref[1], scal_ref[2]
    f_prev, f_own, f_next, base = scal_ref[3], scal_ref[4], scal_ref[5], scal_ref[6]
    slots = slots_ref[...]
    shape = slots.shape
    lane = lax.broadcasted_iota(jnp.int32, shape, 1)
    row = lax.broadcasted_iota(jnp.int32, shape, 0)
    local = lane >> 6
    atom = row * 8 + local + base
    region = slots >> 10
    within = slots & 1023
    filled = jnp.where(region == 0, f_prev, jnp.where(region == 1, f_own, f_next))
    usable = (slots >= 0) & (within < filled) & (atom < f_own)
    kblock = within >> 7
    place = jnp.where(region == 1, 0, jnp.where(region == 2 * odd, 2, 4)) + ((kblock & 1) ^ zh)
    target = jnp.where(usable, ((((kblock >> 1) - y) & 3) * 6 + place) * 8 + local, -1)
    low = slots & 127
    iota_p = lax.broadcasted_iota(jnp.int32, (192, 512), 0)
    iota_l = lax.broadcasted_iota(jnp.int32, (128, 512), 0)
    for i in range(16):
        p = jnp.where(iota_p == target[i : i + 1], 1.0, 0.0).astype(BF16)
        l = jnp.where(iota_l == low[i : i + 1], 1.0, 0.0).astype(BF16)
        c = nt(p, l).reshape(24, 8, 128)
        for j in range(4):
            cnt_refs[j][:, 8 * i : 8 * i + 8, :] = c[6 * j : 6 * j + 6]


def update(gathered, hidden, self_weight):
    drive = gathered * 0.125 + nn(hidden, self_weight)
    return (hidden.astype(F32) + drive * jax.nn.sigmoid(drive)).astype(BF16)


def mix(acc, mixing):
    total = acc[0:ROWS] * mixing[0:1]
    for n in range(1, 8):
        total = total + acc[n * ROWS : (n + 1) * ROWS] * mixing[n : n + 1]
    return total


def block_of(y_ref, c_ref, i):
    return y_ref[i] if i < 4 else c_ref[i - 4]


def basis_block(payload, x_shift, cnt_ref, i, g_ref, here_s):
    xyz = coordinates(payload)
    x = xyz[0:1] + x_shift
    for r in range(0, ROWS, 32):
        dx = x - here_s[0, r : r + 32, :]
        dy = xyz[1:2] - here_s[1, r : r + 32, :]
        dz = xyz[2:3] - here_s[2, r : r + 32, :]
        v = dx * dx + dy * dy + dz * dz + (0.04 - CENTRE)
        cur = cnt_ref[i, r : r + 32, :] * horner(SINC, v)
        turn = horner(TWOCOS, v)
        prev = None
        for n in range(8):
            g_ref[n * ROWS + r : n * ROWS + r + 32, i * 128 : (i + 1) * 128] = cur.astype(BF16)
            if n < 7:
                nxt = turn * cur if prev is None else turn * cur - prev
                prev, cur = cur, nxt


def basis_part(shift_ref, near_ref, z, y_ref, c_ref, cnt_ref, g_ref, here_s):
    xyz = coordinates(near_ref[z])
    for d in range(3):
        here_s[d] = jnp.broadcast_to(xyz[d : d + 1], (128, ROWS)).T

    for i in range(6):
        basis_block(block_of(y_ref, c_ref, i), shift_ref[i // 2], cnt_ref, i, g_ref, here_s)


def messages_of(y_ref, c_ref, weight):
    rows = jnp.concatenate([block_of(y_ref, c_ref, i)[0:ROWS, :] for i in range(6)], axis=0)
    return nn(rows, weight).astype(BF16)


def first_body(shift_ref, near_ref, y_ref, c_ref, cnt_ref, edge_ref, mixing_ref, g_ref, part_ref, here_s):
    messages = messages_of(y_ref, c_ref, edge_ref[0])
    basis_part(shift_ref, near_ref, 0, y_ref, c_ref, cnt_ref, g_ref, here_s)
    part_ref[...] = mix(nn(g_ref[...], messages), mixing_ref[0])


def first_last_body(shift_ref, near_ref, y_ref, c_ref, cnt_ref, edge_ref, mixing_ref, p0, p1, p2, node_ref, g_ref, hidden_ref, here_s):
    messages = messages_of(y_ref, c_ref, edge_ref[0])
    basis_part(shift_ref, near_ref, 0, y_ref, c_ref, cnt_ref, g_ref, here_s)
    gathered = ((p0[...] + p1[...]) + p2[...]) + mix(nn(g_ref[...], messages), mixing_ref[0])
    hidden_ref[...] = update(gathered, near_ref[0, 0:ROWS, :], node_ref[0])


def partner_body(shift_ref, near_ref, y_ref, c_ref, cnt_ref, g_ref, here_s):
    basis_part(shift_ref, near_ref, 1, y_ref, c_ref, cnt_ref, g_ref, here_s)


def second_part(y_ref, c_ref, own_ref, partner_ref, edge_ref, mixing_ref):
    messages = messages_of(y_ref, c_ref, edge_ref[1])
    return [mix(nn(g[...], messages), mixing_ref[1]) for g in (own_ref, partner_ref)]


def second_body(y_ref, c_ref, own_ref, partner_ref, edge_ref, mixing_ref, part_ref):
    for z, part in enumerate(second_part(y_ref, c_ref, own_ref, partner_ref, edge_ref, mixing_ref)):
        part_ref[z] = part


def second_last_body(scal_ref, y_ref, c_ref, own_ref, partner_ref, edge_ref, mixing_ref, p0, p1, p2, near_ref, node_ref, readout_ref, charge_ref):
    for z, part in enumerate(second_part(y_ref, c_ref, own_ref, partner_ref, edge_ref, mixing_ref)):
        gathered = ((p0[z] + p1[z]) + p2[z]) + part
        hidden = update(gathered, near_ref[z], node_ref[1])
        charges = nt(readout_ref[...], hidden)
        atom = lax.broadcasted_iota(jnp.int32, charges.shape, 1) + scal_ref[6 + z]
        charge_ref[z] = jnp.where(atom < scal_ref[4], charges, 0.0)


def copy_body(in_ref, out_ref):
    out_ref[...] = in_ref[...]


def stack_body(a, b, c, d, out_ref):
    for i, ref in enumerate((a, b, c, d)):
        out_ref[i] = ref[...]


def cross(pieces, left):
    hi, mid, lo = [p.astype(F32) for p in pieces]
    rows = [hi, hi, mid, hi, lo, mid] if left else [hi, mid, hi, lo, hi, mid]
    return jnp.concatenate(rows + [jnp.zeros((6, hi.shape[1]), F32)], axis=0)


def modes_body(modes_ref, out_ref):
    turns = modes_ref[...] * (0.5 / math.pi)
    out_ref[...] = cross(split(turns, 3), True).T.astype(BF16)


def phase_body(y_ref, modes_ref, wave_ref):
    for b in range(2):
        places = cross(split(coordinates(y_ref[b]), 3), False).astype(BF16)
        for r in range(0, 1024, 64):
            turns = nn(modes_ref[r : r + 64, :], places)
            rest = turns - jnp.round(turns)
            square = rest * rest
            wave_ref[r : r + 64, b * 128 : (b + 1) * 128] = horner(COSTURN, square).astype(BF16)
            wave_ref[r + 1024 : r + 1088, b * 128 : (b + 1) * 128] = (rest * horner(SINTURN, square)).astype(BF16)


def half_of(ref, half, sine):
    return ref[pl.ds(pl.multiple_of(half * 512 + sine * 1024, 512), 512), :]


def structure_body(half_ref, w0, w1, w2, w3, q0, q1, q2, q3, mine_ref, theirs_ref):
    pieces = [jnp.concatenate(split(jnp.concatenate([q[0], q[1]], axis=1), 3), axis=0) for q in (q0, q1, q2, q3)]
    for half, out_ref in ((1 - half_ref[0], theirs_ref), (half_ref[0], mine_ref)):
        for i in range(2):
            s = None
            for p, w in zip(pieces, (w0, w1, w2, w3)):
                term = nt(p, half_of(w, half, i))
                s = term if s is None else s + term
            out_ref[16 * i : 16 * i + 16, :] = s[0:16] + s[16:32] + s[32:48]


def respond_body(half_ref, place_ref, scale_ref, w0, w1, w2, w3, q0, q1, q2, q3, mine_ref, theirs_ref, modes_ref, out_ref):
    k = modes_ref[...]
    square = k[0:1] * k[0:1] + k[1:2] * k[1:2] + k[2:3] * k[2:3]
    weight = scale_ref[0] * jnp.exp(square * -0.125) / (square + 1.0)
    low = jnp.where(half_ref[0] == 0, mine_ref[...], theirs_ref[...])
    high = jnp.where(half_ref[0] == 0, theirs_ref[...], mine_ref[...])
    total = jnp.concatenate([low, high], axis=1) * weight
    real, imag = total[0:16], total[16:32]
    left = [real] + [imag * k[j : j + 1] for j in range(3)]
    right = [imag] + [real * -k[j : j + 1] for j in range(3)]
    both = jnp.concatenate([jnp.concatenate(left, axis=0), jnp.concatenate(right, axis=0)], axis=1)
    pieces = jnp.concatenate(split(both, 2), axis=0)
    for i, (w, q) in enumerate(zip((w0, w1, w2, w3), (q0, q1, q2, q3))):
        out = nn(pieces, w[...])
        out = out[0:64] + out[64:128]
        for b in range(2):
            mine = out[:, b * 128 : (b + 1) * 128]
            force = [-jnp.sum(mine[16 * j + 16 : 16 * j + 32] * q[b], axis=0, keepdims=True) for j in range(3)]
            out_ref[place_ref[2 * i + b]] = jnp.concatenate([mine[0:16]] + force + [jnp.zeros((5, 128), F32)], axis=0)


def finish_body(parts_ref, potential_ref, forces_ref):
    total = parts_ref[0]
    for i in range(1, 8):
        total = total + parts_ref[i]
    potential_ref[...] = total[0:16]
    forces_ref[...] = total[16:19]


def pairs(n_slab, target):
    return [(s * 8 + k, (target(s, k)[0] % n_slab) * 8 + target(s, k)[1]) for s in range(n_slab) for k in range(8)]


def move(x, target):
    return lax.ppermute(x, AXES, pairs(lax.axis_size("slab"), target))


def over_chip(s):
    return s + 1 if s % 2 else s - 1


def near_blocks(block):
    half = move(block, lambda s, k: (s, k ^ 1))
    near = move(block, lambda s, k: (over_chip(s), k))
    both = move(block, lambda s, k: (over_chip(s), k ^ 1))
    return half, near, both


def surroundings(block, near, name, after):
    stack = call(stack_body, jax.ShapeDtypeStruct((4,) + block.shape, BF16), block, *near, name=name, after=after)
    ys = [stack]
    for j in range(1, 4):
        ys.append(move(stack, lambda s, k: (s, (k - 2 * j) % 8)))
    return ys, [move(y[0:2], lambda s, k: (s ^ 1, k)) for y in ys]


def shards(
    atom_descriptors,
    atom_locations,
    adjacent_atom_slots,
    neighbour_tally,
    filled_slot_tallies,
    reciprocal_lattice_modes,
    edge_update_matrix,
    node_update_matrix,
    distance_basis_mixing,
    latent_ionic_readout,
):
    n_slab = lax.axis_size("slab")
    slab = lax.axis_index("slab")
    group = lax.axis_index("kgrp")
    odd = slab % 2
    y, zh = group // 2, group % 2
    filled = jnp.take(filled_slot_tallies, (slab + jnp.arange(3) - 1) % n_slab)
    scal = jnp.concatenate([jnp.stack([y, zh, odd]), filled, jnp.stack([group * ROWS, (group ^ 1) * ROWS])]).astype(jnp.int32)
    low_edge = jnp.where(slab == 0, -float(n_slab), 0.0)
    high_edge = jnp.where(slab == n_slab - 1, float(n_slab), 0.0)
    shift = jnp.stack([0.0, jnp.where(odd == 1, high_edge, low_edge), jnp.where(odd == 1, low_edge, high_edge)]).astype(F32)
    spots = jnp.arange(8, dtype=jnp.int32)
    place = (((y + spots // 2) % 4) * 2 + ((spots % 2) ^ zh)).astype(jnp.int32)

    shape = jax.ShapeDtypeStruct
    block = call(pack_body, shape((PAYLOAD, ROWS), BF16), atom_descriptors, atom_locations, name="pack")
    near = near_blocks(block)
    used = jnp.arange(64, dtype=jnp.int32)[None, :] < neighbour_tally[:, None]
    slots = jnp.where(used, adjacent_atom_slots, -1).reshape(16, 512)

    def count(slots, base, name, after=()):
        bounds = jnp.concatenate([scal[:6], scal[base : base + 1]])
        return call(count_body, [shape((6, ROWS, 128), F32)] * 4, slots, scalars=(bounds,), name=name, flops=10**9, after=after)

    counts = count(slots, 6, "counts")
    ys, cs = surroundings(block, near, "stack_first", (counts[0],))
    late = call(copy_body, shape((16, 512), jnp.int32), slots, name="late", after=(cs[0],))
    partner_slots = move(late, lambda s, k: (s, k ^ 1))
    wide = shape((8 * ROWS, 6 * ROWS), BF16)
    here = [pltpu.VMEM((3, ROWS, 128), F32)]
    basis, parts = [None] * 4, [None] * 3
    for j in range(3):
        basis[j], parts[j] = call(
            first_body, (wide, shape((ROWS, 128), F32)),
            ys[0], ys[j], cs[j], counts[j], edge_update_matrix, distance_basis_mixing,
            scalars=(shift,), name=f"first_{j}", flops=10**9, scratch=here,
        )
    basis[3], hidden = call(
        first_last_body, (wide, shape((ROWS, 128), BF16)),
        ys[0], ys[3], cs[3], counts[3], edge_update_matrix, distance_basis_mixing, *parts, node_update_matrix,
        scalars=(shift,), name="first_3", flops=10**9, scratch=here, after=(partner_slots,),
    )
    partner_counts = count(partner_slots, 7, "partner_counts", (hidden,))
    turns = call(modes_body, shape((1024, 24), BF16), reciprocal_lattice_modes, name="modes")

    def phases(j, after):
        return call(phase_body, shape((2048, 256), BF16), ys[j], turns, name=f"phases_{j}", flops=10**9, after=after)

    def partner_basis(j, after):
        return call(
            partner_body, wide, ys[0], ys[j], cs[j], partner_counts[j],
            scalars=(shift,), name=f"partner_{j}", flops=10**9, scratch=here, after=after,
        )

    near = near_blocks(hidden)
    partner = [partner_basis(j, (hidden,)) for j in range(2)]
    ms, ns = surroundings(hidden, near, "stack_second", partner)
    partner += [partner_basis(j, (ms[0],)) for j in range(2, 4)]
    waves = [phases(j, (ms[0],)) for j in range(2)]
    parts = [
        call(
            second_body, shape((2, ROWS, 128), F32),
            ms[j], ns[j], basis[j], partner[j], edge_update_matrix, distance_basis_mixing,
            name=f"second_{j}", flops=10**9, after=partner[2:] + waves if j == 0 else (),
        )
        for j in range(3)
    ]
    charges = call(
        second_last_body, shape((2, 16, ROWS), F32),
        ms[3], ns[3], basis[3], partner[3], edge_update_matrix, distance_basis_mixing, *parts, ms[0], node_update_matrix, latent_ionic_readout.T,
        scalars=(scal,), name="second_3", flops=10**9,
    )
    qs = [charges] + [move(charges, lambda s, k, j=j: (s, (k - 2 * j) % 8)) for j in range(1, 4)]
    waves += [phases(j, (charges,)) for j in range(2, 4)]
    mine = jnp.reshape(odd, (1,)).astype(jnp.int32)
    part, away = call(
        structure_body, (shape((32, 512), F32), shape((32, 512), F32)), *waves, *qs,
        scalars=(mine,), name="structure", flops=10**8,
    )
    part = part + move(away, lambda s, k: (s ^ 1, k))
    half = part.astype(BF16)
    part = part + sum(move(half, lambda s, k, m=m: (s + 8 * m, k)).astype(F32) for m in (1, 2, 3))
    half = part.astype(BF16)
    part = part + sum(move(half, lambda s, k, m=m: (s ^ (2 * m), k)).astype(F32) for m in (1, 2, 3))
    other = move(part, lambda s, k: (s ^ 1, k))
    scale = jnp.full((1,), 4.0 / math.sqrt(n_slab * 1024 * reciprocal_lattice_modes.shape[1] * 8), F32)
    partial = call(
        respond_body, shape((8, 24, ROWS), F32), *waves, *qs, part, other, reciprocal_lattice_modes,
        scalars=(mine, place, scale), name="respond", flops=10**8,
    )
    partial = lax.all_to_all(partial, "kgrp", 0, 0)
    return tuple(call(finish_body, (shape((16, ROWS), F32), shape((3, ROWS), F32)), partial, name="finish"))


def solution(mesh):
    return jax.shard_map(
        shards,
        mesh=mesh,
        in_specs=(
            P(("slab", "kgrp"), None),
            P(None, ("slab", "kgrp")),
            P(("slab", "kgrp"), None),
            P(("slab", "kgrp")),
            P(),
            P(None, "kgrp"),
            P(),
            P(),
            P(),
            P(),
        ),
        out_specs=(P(None, ("slab", "kgrp")), P(None, ("slab", "kgrp"))),
        check_vma=False,
    )
```

```python
import math

import jax
import jax.numpy as jnp
from jax import lax
from jax.experimental import pallas as pl
from jax.experimental.pallas import tpu as pltpu
from jax.sharding import PartitionSpec as P

AXES = ("slab", "kgrp")
F32 = jnp.float32
BF16 = jnp.bfloat16
MIB = 1 << 20

ROWS = 128
PAYLOAD = 144
HALF = 64

CENTRE = 3.04
SINC = (0.4531433647, -0.11001027431, 0.0067080034928, -0.00018563842882, 2.9260279482e-06)
TWOCOS = (-0.504597100576, -0.581178942324, 0.0705470232447, -0.0028677843003, 5.9501086291e-05, -7.504320417652e-07)
SINTURN = (6.283184916495, -41.341589232689, 81.599943329776, -76.614472532619, 41.342882354378, -12.471243534759)
COSTURN = (0.99999921078, -19.738980355764, 64.92865742103, -85.271621534265, 58.790492119989, -21.071105627427)


def horner(coefficients, x):
    value = coefficients[-1] * x + coefficients[-2]
    for c in coefficients[-3::-1]:
        value = value * x + c
    return value


def split(x, parts):
    pieces = []
    for i in range(parts):
        piece = x.astype(BF16)
        pieces.append(piece)
        if i + 1 < parts:
            x = x - piece.astype(F32)
    return pieces


def nt(a, b):
    return lax.dot_general(a, b, (((1,), (1,)), ((), ())), preferred_element_type=F32)


def nn(a, b):
    return jnp.dot(a, b, preferred_element_type=F32)


def call(body, out_shape, *operands, scalars=(), after=(), name, flops=0, limit=12, scratch=()):
    n, m = len(scalars) + len(operands), len(after)
    return pl.pallas_call(
        lambda *refs: body(*refs[:n], *refs[n + m :]),
        out_shape=out_shape,
        in_specs=[pl.BlockSpec(memory_space=pltpu.SMEM)] * len(scalars)
        + [pl.BlockSpec(memory_space=pltpu.VMEM)] * len(operands)
        + [pl.BlockSpec(memory_space=pl.ANY)] * m,
        scratch_shapes=list(scratch),
        name=name,
        cost_estimate=pl.CostEstimate(flops=flops, bytes_accessed=MIB, transcendentals=0),
        compiler_params=pltpu.CompilerParams(vmem_limit_bytes=limit * MIB),
    )(*scalars, *operands, *after)


def pack_body(desc_ref, loc_ref, out_ref):
    out_ref[0:ROWS, :] = desc_ref[...]
    hi, mid, lo = [p.astype(F32) for p in split(loc_ref[...], 3)]
    tail = jnp.concatenate([hi, mid, lo, jnp.zeros((7, ROWS), F32)], axis=0)
    out_ref[ROWS:PAYLOAD, :] = tail.astype(BF16)


def coordinates(payload):
    tail = payload[ROWS:PAYLOAD, :].astype(F32)
    return (tail[0:3] + tail[3:6]) + tail[6:9]


def count_body(scal_ref, slots_ref, cnt0, cnt1, cnt2, cnt3, target_s, low_s):
    y, zh, odd = scal_ref[0], scal_ref[1], scal_ref[2]
    f_prev, f_own, f_next, base = scal_ref[3], scal_ref[4], scal_ref[5], scal_ref[6]
    slots = slots_ref[...]
    shape = slots.shape
    lane = lax.broadcasted_iota(jnp.int32, shape, 1)
    row = lax.broadcasted_iota(jnp.int32, shape, 0)
    local = lane >> 6
    atom = row * 8 + local + base
    region = slots >> 10
    within = slots & 1023
    filled = jnp.where(region == 0, f_prev, jnp.where(region == 1, f_own, f_next))
    usable = (slots >= 0) & (within < filled) & (atom < f_own)
    kblock = within >> 7
    place = jnp.where(region == 1, 0, jnp.where(region == 2 * odd, 2, 4)) + ((kblock & 1) ^ zh)
    target = jnp.where(usable, ((((kblock >> 1) - y) & 3) * 6 + place) * 8 + local, -1)
    target_s[...] = target
    low_s[...] = slots & 127
    iota_p = lax.broadcasted_iota(jnp.int32, (192, 512), 0)
    iota_l = lax.broadcasted_iota(jnp.int32, (128, 512), 0)

    @pl.loop(0, 4)
    def _(step):
        for u in range(4):
            i = step * 4 + u
            p = jnp.where(iota_p == target_s[pl.ds(i, 1), :], 1.0, 0.0).astype(BF16)
            l = jnp.where(iota_l == low_s[pl.ds(i, 1), :], 1.0, 0.0).astype(BF16)
            c = nt(p, l).reshape(24, 8, 128)
            for j, cnt_ref in enumerate((cnt0, cnt1, cnt2, cnt3)):
                cnt_ref[:, pl.ds(pl.multiple_of(8 * i, 8), 8), :] = c[6 * j : 6 * j + 6]


def update(gathered, hidden, self_weight):
    drive = gathered * 0.125 + nn(hidden, self_weight)
    return (hidden.astype(F32) + drive * jax.nn.sigmoid(drive)).astype(BF16)


def mix(acc, mixing):
    total = acc[0:HALF] * mixing[0:1]
    for n in range(1, 8):
        total = total + acc[n * HALF : (n + 1) * HALF] * mixing[n : n + 1]
    return total


def rows_of(h, count):
    return pl.ds(pl.multiple_of(h * count, count), count)


def block_of(y_ref, c_ref, i):
    return y_ref[i] if i < 4 else c_ref[i - 4]


def here_of(near_ref, z, here_s):
    xyz = coordinates(near_ref[z])
    for d in range(3):
        here_s[d] = jnp.broadcast_to(xyz[d : d + 1], (128, ROWS)).T


def basis_half(h, shift_ref, y_ref, c_ref, cnt_ref, g_ref, here_s):
    for i in range(6):
        xyz = coordinates(block_of(y_ref, c_ref, i))
        x = xyz[0:1] + shift_ref[i // 2]
        for r in range(0, HALF, 32):
            rows = pl.ds(pl.multiple_of(h * HALF + r, 32), 32)
            dx = x - here_s[0, rows, :]
            dy = xyz[1:2] - here_s[1, rows, :]
            dz = xyz[2:3] - here_s[2, rows, :]
            v = dx * dx + dy * dy + dz * dz + (0.04 - CENTRE)
            cur = cnt_ref[i, rows, :] * horner(SINC, v)
            turn = horner(TWOCOS, v)
            prev = None
            for n in range(8):
                g_ref[pl.ds(pl.multiple_of(h * 512 + n * HALF + r, 32), 32), i * 128 : (i + 1) * 128] = cur.astype(BF16)
                if n < 7:
                    nxt = turn * cur if prev is None else turn * cur - prev
                    prev, cur = cur, nxt


def messages_of(y_ref, c_ref, weight):
    rows = jnp.concatenate([block_of(y_ref, c_ref, i)[0:ROWS, :] for i in range(6)], axis=0)
    return nn(rows, weight).astype(BF16)


def first_body(shift_ref, y_ref, c_ref, cnt_ref, edge_ref, mixing_ref, g_ref, part_ref, here_s, messages_s):
    messages_s[...] = messages_of(y_ref, c_ref, edge_ref[0])
    here_of(y_ref, 0, here_s)

    @pl.loop(0, 2)
    def _(h):
        basis_half(h, shift_ref, y_ref, c_ref, cnt_ref, g_ref, here_s)
        part_ref[rows_of(h, HALF), :] = mix(nn(g_ref[rows_of(h, 512), :], messages_s[...]), mixing_ref[0])


def first_rest_body(shift_ref, near_ref, y1, y2, y3, c1, c2, c3, n1, n2, n3, edge_ref, mixing_ref, part_ref, node_ref, g1, g2, g3, hidden_ref, here_s, messages_s, total_s):
    for j, (y, c) in enumerate(((y1, c1), (y2, c2), (y3, c3))):
        messages_s[j] = messages_of(y, c, edge_ref[0])
    here_of(near_ref, 0, here_s)

    @pl.loop(0, 2)
    def _(h):
        acc = None
        for j, (y, c, n, g) in enumerate(((y1, c1, n1, g1), (y2, c2, n2, g2), (y3, c3, n3, g3))):
            basis_half(h, shift_ref, y, c, n, g, here_s)
            term = nn(g[rows_of(h, 512), :], messages_s[j])
            acc = term if acc is None else acc + term
        total_s[rows_of(h, HALF), :] = mix(acc, mixing_ref[0])

    hidden_ref[...] = update(part_ref[...] + total_s[...], near_ref[0, 0:ROWS, :], node_ref[0])


def partner_body(shift_ref, near_ref, ya, yb, ca, cb, na, nb, ga, gb, here_s):
    here_of(near_ref, 1, here_s)

    @pl.loop(0, 2)
    def _(h):
        basis_half(h, shift_ref, ya, ca, na, ga, here_s)
        basis_half(h, shift_ref, yb, cb, nb, gb, here_s)


def second_body(y_ref, c_ref, own_ref, partner_ref, edge_ref, mixing_ref, part_ref, messages_s):
    messages_s[...] = messages_of(y_ref, c_ref, edge_ref[1])

    @pl.loop(0, 2)
    def _(h):
        for z, g in enumerate((own_ref, partner_ref)):
            part_ref[z, rows_of(h, HALF), :] = mix(nn(g[rows_of(h, 512), :], messages_s[...]), mixing_ref[1])


def second_rest_body(scal_ref, y1, y2, y3, c1, c2, c3, o1, o2, o3, p1, p2, p3, edge_ref, mixing_ref, part_ref, near_ref, node_ref, readout_ref, charge_ref, messages_s, total_s):
    for j, (y, c) in enumerate(((y1, c1), (y2, c2), (y3, c3))):
        messages_s[j] = messages_of(y, c, edge_ref[1])

    @pl.loop(0, 2)
    def _(h):
        for z, gs in enumerate(((o1, o2, o3), (p1, p2, p3))):
            acc = None
            for j, g in enumerate(gs):
                term = nn(g[rows_of(h, 512), :], messages_s[j])
                acc = term if acc is None else acc + term
            total_s[z, rows_of(h, HALF), :] = mix(acc, mixing_ref[1])

    for z in range(2):
        hidden = update(part_ref[z] + total_s[z], near_ref[z], node_ref[1])
        charges = nt(readout_ref[...], hidden)
        atom = lax.broadcasted_iota(jnp.int32, charges.shape, 1) + scal_ref[6 + z]
        charge_ref[z] = jnp.where(atom < scal_ref[4], charges, 0.0)


def copy_body(in_ref, out_ref):
    out_ref[...] = in_ref[...]


def stack_body(a, b, c, d, out_ref):
    for i, ref in enumerate((a, b, c, d)):
        out_ref[i] = ref[...]


def cross(pieces, left):
    hi, mid, lo = [p.astype(F32) for p in pieces]
    rows = [hi, hi, mid, hi, lo, mid] if left else [hi, mid, hi, lo, hi, mid]
    return jnp.concatenate(rows + [jnp.zeros((6, hi.shape[1]), F32)], axis=0)


def modes_body(modes_ref, out_ref):
    turns = modes_ref[...] * (0.5 / math.pi)
    out_ref[...] = cross(split(turns, 3), True).T.astype(BF16)


def phase_body(y_ref, modes_ref, wave_ref):

    @pl.loop(0, 2)
    def _(b):
        places = cross(split(coordinates(y_ref[b]), 3), False).astype(BF16)
        columns = pl.ds(pl.multiple_of(b * 128, 128), 128)
        for r in range(0, 1024, 64):
            turns = nn(modes_ref[r : r + 64, :], places)
            rest = turns - jnp.round(turns)
            square = rest * rest
            wave_ref[r : r + 64, columns] = horner(COSTURN, square).astype(BF16)
            wave_ref[r + 1024 : r + 1088, columns] = (rest * horner(SINTURN, square)).astype(BF16)


def half_of(ref, half, sine):
    return ref[pl.ds(pl.multiple_of(half * 512 + sine * 1024, 512), 512), :]


def structure_body(half_ref, w0, w1, w2, w3, q0, q1, q2, q3, mine_ref, theirs_ref):
    pieces = [jnp.concatenate(split(jnp.concatenate([q[0], q[1]], axis=1), 3), axis=0) for q in (q0, q1, q2, q3)]
    for half, out_ref in ((1 - half_ref[0], theirs_ref), (half_ref[0], mine_ref)):
        for i in range(2):
            s = None
            for p, w in zip(pieces, (w0, w1, w2, w3)):
                term = nt(p, half_of(w, half, i))
                s = term if s is None else s + term
            out_ref[16 * i : 16 * i + 16, :] = s[0:16] + s[16:32] + s[32:48]


def respond_body(half_ref, place_ref, scale_ref, w0, w1, w2, w3, q0, q1, q2, q3, mine_ref, theirs_ref, modes_ref, out_ref):
    k = modes_ref[...]
    square = k[0:1] * k[0:1] + k[1:2] * k[1:2] + k[2:3] * k[2:3]
    weight = scale_ref[0] * jnp.exp(square * -0.125) / (square + 1.0)
    low = jnp.where(half_ref[0] == 0, mine_ref[...], theirs_ref[...])
    high = jnp.where(half_ref[0] == 0, theirs_ref[...], mine_ref[...])
    total = jnp.concatenate([low, high], axis=1) * weight
    real, imag = total[0:16], total[16:32]
    left = [real] + [imag * k[j : j + 1] for j in range(3)]
    right = [imag] + [real * -k[j : j + 1] for j in range(3)]
    both = jnp.concatenate([jnp.concatenate(left, axis=0), jnp.concatenate(right, axis=0)], axis=1)
    pieces = jnp.concatenate(split(both, 2), axis=0)
    for i, (w, q) in enumerate(zip((w0, w1, w2, w3), (q0, q1, q2, q3))):
        out = nn(pieces, w[...])
        out = out[0:64] + out[64:128]
        for b in range(2):
            mine = out[:, b * 128 : (b + 1) * 128]
            force = [-jnp.sum(mine[16 * j + 16 : 16 * j + 32] * q[b], axis=0, keepdims=True) for j in range(3)]
            out_ref[place_ref[2 * i + b]] = jnp.concatenate([mine[0:16]] + force + [jnp.zeros((5, 128), F32)], axis=0)


def finish_body(parts_ref, potential_ref, forces_ref):
    total = parts_ref[0]
    for i in range(1, 8):
        total = total + parts_ref[i]
    potential_ref[...] = total[0:16]
    forces_ref[...] = total[16:19]


def pairs(n_slab, target):
    return [(s * 8 + k, (target(s, k)[0] % n_slab) * 8 + target(s, k)[1]) for s in range(n_slab) for k in range(8)]


def move(x, target):
    return lax.ppermute(x, AXES, pairs(lax.axis_size("slab"), target))


def over_chip(s):
    return s + 1 if s % 2 else s - 1


def near_blocks(block):
    half = move(block, lambda s, k: (s, k ^ 1))
    near = move(block, lambda s, k: (over_chip(s), k))
    both = move(block, lambda s, k: (over_chip(s), k ^ 1))
    return half, near, both


def surroundings(block, near, name, after):
    stack = call(stack_body, jax.ShapeDtypeStruct((4,) + block.shape, BF16), block, *near, name=name, after=after)
    ys = [stack]
    for j in range(1, 4):
        ys.append(move(stack, lambda s, k: (s, (k - 2 * j) % 8)))
    return ys, [move(y[0:2], lambda s, k: (s ^ 1, k)) for y in ys]


def shards(
    atom_descriptors,
    atom_locations,
    adjacent_atom_slots,
    neighbour_tally,
    filled_slot_tallies,
    reciprocal_lattice_modes,
    edge_update_matrix,
    node_update_matrix,
    distance_basis_mixing,
    latent_ionic_readout,
):
    n_slab = lax.axis_size("slab")
    slab = lax.axis_index("slab")
    group = lax.axis_index("kgrp")
    odd = slab % 2
    y, zh = group // 2, group % 2
    filled = jnp.take(filled_slot_tallies, (slab + jnp.arange(3) - 1) % n_slab)
    scal = jnp.concatenate([jnp.stack([y, zh, odd]), filled, jnp.stack([group * ROWS, (group ^ 1) * ROWS])]).astype(jnp.int32)
    low_edge = jnp.where(slab == 0, -float(n_slab), 0.0)
    high_edge = jnp.where(slab == n_slab - 1, float(n_slab), 0.0)
    shift = jnp.stack([0.0, jnp.where(odd == 1, high_edge, low_edge), jnp.where(odd == 1, low_edge, high_edge)]).astype(F32)
    spots = jnp.arange(8, dtype=jnp.int32)
    place = (((y + spots // 2) % 4) * 2 + ((spots % 2) ^ zh)).astype(jnp.int32)

    shape = jax.ShapeDtypeStruct
    block = call(pack_body, shape((PAYLOAD, ROWS), BF16), atom_descriptors, atom_locations, name="pack")
    near = near_blocks(block)
    used = jnp.arange(64, dtype=jnp.int32)[None, :] < neighbour_tally[:, None]
    slots = jnp.where(used, adjacent_atom_slots, -1).reshape(16, 512)

    def count(slots, base, name, after=()):
        bounds = jnp.concatenate([scal[:6], scal[base : base + 1]])
        return call(
            count_body, [shape((6, ROWS, 128), F32)] * 4, slots, scalars=(bounds,), name=name, flops=10**9, after=after,
            scratch=[pltpu.VMEM((16, 512), jnp.int32)] * 2,
        )

    counts = count(slots, 6, "counts")
    ys, cs = surroundings(block, near, "stack_first", (counts[0],))
    late = call(copy_body, shape((16, 512), jnp.int32), slots, name="late", after=(cs[0],))
    partner_slots = move(late, lambda s, k: (s, k ^ 1))
    wide = shape((8 * ROWS, 6 * ROWS), BF16)
    here = pltpu.VMEM((3, ROWS, 128), F32)
    message = lambda *n: pltpu.VMEM(n + (6 * ROWS, 128), BF16)
    basis = [None] * 4
    basis[0], part = call(
        first_body, (wide, shape((ROWS, 128), F32)),
        ys[0], cs[0], counts[0], edge_update_matrix, distance_basis_mixing,
        scalars=(shift,), name="first_0", flops=10**9, scratch=[here, message()],
    )
    basis[1], basis[2], basis[3], hidden = call(
        first_rest_body, (wide, wide, wide, shape((ROWS, 128), BF16)),
        *ys, *cs[1:], *counts[1:], edge_update_matrix, distance_basis_mixing, part, node_update_matrix,
        scalars=(shift,), name="first_rest", flops=10**9, scratch=[here, message(3), pltpu.VMEM((ROWS, 128), F32)], after=(partner_slots,),
    )
    partner_counts = count(partner_slots, 7, "partner_counts", (hidden,))
    turns = call(modes_body, shape((1024, 24), BF16), reciprocal_lattice_modes, name="modes")

    def phases(j, after):
        return call(phase_body, shape((2048, 256), BF16), ys[j], turns, name=f"phases_{j}", flops=10**9, after=after)

    def partner_basis(a, b, after):
        return call(
            partner_body, [wide, wide], ys[0], ys[a], ys[b], cs[a], cs[b], partner_counts[a], partner_counts[b],
            scalars=(shift,), name=f"partner_{a}", flops=10**9, scratch=[here], after=after,
        )

    near = near_blocks(hidden)
    partner = [*partner_basis(0, 1, (hidden,))]
    ms, ns = surroundings(hidden, near, "stack_second", partner[:1])
    partner += [*partner_basis(2, 3, (ms[0],))]
    waves = [phases(j, (ms[0],)) for j in range(2)]
    part = call(
        second_body, shape((2, ROWS, 128), F32),
        ms[0], ns[0], basis[0], partner[0], edge_update_matrix, distance_basis_mixing,
        name="second_0", flops=10**9, scratch=[message()], after=[partner[2], *waves],
    )
    charges = call(
        second_rest_body, shape((2, 16, ROWS), F32),
        *ms[1:], *ns[1:], *basis[1:], *partner[1:], edge_update_matrix, distance_basis_mixing, part, ms[0], node_update_matrix, latent_ionic_readout.T,
        scalars=(scal,), name="second_rest", flops=10**9, scratch=[message(3), pltpu.VMEM((2, ROWS, 128), F32)],
    )
    qs = [charges] + [move(charges, lambda s, k, j=j: (s, (k - 2 * j) % 8)) for j in range(1, 4)]
    waves += [phases(j, (charges,)) for j in range(2, 4)]
    mine = jnp.reshape(odd, (1,)).astype(jnp.int32)
    part, away = call(
        structure_body, (shape((32, 512), F32), shape((32, 512), F32)), *waves, *qs,
        scalars=(mine,), name="structure", flops=10**8,
    )
    part = part + move(away, lambda s, k: (s ^ 1, k))
    half = part.astype(BF16)
    part = part + sum(move(half, lambda s, k, m=m: (s + 8 * m, k)).astype(F32) for m in (1, 2, 3))
    half = part.astype(BF16)
    part = part + sum(move(half, lambda s, k, m=m: (s ^ (2 * m), k)).astype(F32) for m in (1, 2, 3))
    other = move(part, lambda s, k: (s ^ 1, k))
    scale = jnp.full((1,), 4.0 / math.sqrt(n_slab * 1024 * reciprocal_lattice_modes.shape[1] * 8), F32)
    partial = call(
        respond_body, shape((8, 24, ROWS), F32), *waves, *qs, part, other, reciprocal_lattice_modes,
        scalars=(mine, place, scale), name="respond", flops=10**8,
    )
    partial = lax.all_to_all(partial, "kgrp", 0, 0)
    return tuple(call(finish_body, (shape((16, ROWS), F32), shape((3, ROWS), F32)), partial, name="finish"))


def solution(mesh):
    return jax.shard_map(
        shards,
        mesh=mesh,
        in_specs=(
            P(("slab", "kgrp"), None),
            P(None, ("slab", "kgrp")),
            P(("slab", "kgrp"), None),
            P(("slab", "kgrp")),
            P(),
            P(None, "kgrp"),
            P(),
            P(),
            P(),
            P(),
        ),
        out_specs=(P(None, ("slab", "kgrp")), P(None, ("slab", "kgrp"))),
        check_vma=False,
    )
```

```python
import functools
import math

import jax
import jax.numpy as jnp
from jax import lax
from jax.experimental import pallas as pl
from jax.experimental.pallas import tpu as pltpu
from jax.sharding import PartitionSpec as P

AXES = ("slab", "kgrp")
F32 = jnp.float32
BF16 = jnp.bfloat16
MIB = 1 << 20

ROWS = 128
PAYLOAD = 144
HALF = 64
WIDE = PAYLOAD + 128

Y, ZH, ODD, F_PREV, F_OWN, F_NEXT, BASE, BASE_PARTNER, PLACE = 0, 1, 2, 3, 4, 5, 6, 7, 8

CENTRE = 3.04
SINC = (0.4531433647, -0.11001027431, 0.0067080034928, -0.00018563842882, 2.9260279482e-06)
TWOCOS = (-0.504597100576, -0.581178942324, 0.0705470232447, -0.0028677843003, 5.9501086291e-05, -7.504320417652e-07)
SINTURN = (6.283184916495, -41.341589232689, 81.599943329776, -76.614472532619, 41.342882354378, -12.471243534759)
COSTURN = (0.99999921078, -19.738980355764, 64.92865742103, -85.271621534265, 58.790492119989, -21.071105627427)


def horner(coefficients, x):
    value = coefficients[-1] * x + coefficients[-2]
    for c in coefficients[-3::-1]:
        value = value * x + c
    return value


def split(x, parts):
    pieces = []
    for i in range(parts):
        piece = x.astype(BF16)
        pieces.append(piece)
        if i + 1 < parts:
            x = x - piece.astype(F32)
    return pieces


def nt(a, b):
    return lax.dot_general(a, b, (((1,), (1,)), ((), ())), preferred_element_type=F32)


def nn(a, b):
    return jnp.dot(a, b, preferred_element_type=F32)


def call(body, out_shape, *operands, scalars=(), after=(), name, flops=0, limit=12, scratch=(), **kw):
    n, m = len(scalars) + len(operands), len(after)
    return pl.pallas_call(
        lambda *refs: body(*refs[:n], *refs[n + m :]),
        out_shape=out_shape,
        in_specs=[pl.BlockSpec(memory_space=pltpu.SMEM)] * len(scalars)
        + [pl.BlockSpec(memory_space=pltpu.VMEM)] * len(operands)
        + [pl.BlockSpec(memory_space=pl.ANY)] * m,
        scratch_shapes=list(scratch),
        name=name,
        cost_estimate=pl.CostEstimate(flops=flops, bytes_accessed=MIB, transcendentals=0),
        compiler_params=pltpu.CompilerParams(vmem_limit_bytes=limit * MIB),
        **kw,
    )(*scalars, *operands, *after)


def pack_body(desc_ref, loc_ref, slots_ref, tally_ref, out_ref, wide_ref):
    hi, mid, lo = [p.astype(F32) for p in split(loc_ref[...], 3)]
    tail = jnp.concatenate([hi, mid, lo, jnp.zeros((7, ROWS), F32)], axis=0).astype(BF16)
    for ref in (out_ref, wide_ref):
        ref[0:ROWS, :] = desc_ref[...]
        ref[ROWS:PAYLOAD, :] = tail
    slots = slots_ref[...]
    used = lax.broadcasted_iota(jnp.int32, slots.shape, 0) < tally_ref[...]
    wide_ref[PAYLOAD : PAYLOAD + 64, :] = jnp.where(used, slots >> 7, -1).astype(F32).astype(BF16)
    wide_ref[PAYLOAD + 64 : WIDE, :] = (slots & 127).astype(F32).astype(BF16)


def layout_body(where_ref, filled_ref, scal_ref, shift_ref, odd_ref):
    slab, group = where_ref[0], where_ref[1]
    n_slab = filled_ref.shape[0]
    y, zh, odd = group >> 1, group & 1, slab & 1
    before = jnp.where(slab == 0, n_slab - 1, slab - 1)
    behind = jnp.where(slab == n_slab - 1, 0, slab + 1)
    scal_ref[Y] = y
    scal_ref[ZH] = zh
    scal_ref[ODD] = odd
    scal_ref[F_PREV] = filled_ref[before]
    scal_ref[F_OWN] = filled_ref[slab]
    scal_ref[F_NEXT] = filled_ref[behind]
    scal_ref[BASE] = group * ROWS
    scal_ref[BASE_PARTNER] = (group ^ 1) * ROWS
    for i in range(8):
        scal_ref[PLACE + i] = (((y + i // 2) & 3) << 1) | ((i % 2) ^ zh)
    low_edge = jnp.where(slab == 0, -float(n_slab), 0.0)
    high_edge = jnp.where(slab == n_slab - 1, float(n_slab), 0.0)
    shift_ref[0] = 0.0
    shift_ref[1] = jnp.where(odd == 1, high_edge, low_edge)
    shift_ref[2] = jnp.where(odd == 1, low_edge, high_edge)
    odd_ref[...] = jnp.full((1, 512), odd, jnp.int32)


def coordinates(payload):
    tail = payload[ROWS:PAYLOAD, :].astype(F32)
    return (tail[0:3] + tail[3:6]) + tail[6:9]


def count_body(which, scal_ref, wide_ref, cnt0, cnt1, cnt2, cnt3):
    y, zh, odd = scal_ref[Y], scal_ref[ZH], scal_ref[ODD]
    f_prev, f_own, f_next, base = scal_ref[F_PREV], scal_ref[F_OWN], scal_ref[F_NEXT], scal_ref[which]

    def paired(rows):
        t = rows.astype(F32).T
        return jnp.concatenate([t[0:64], t[64:128]], axis=1).astype(jnp.int32)

    blocks = paired(wide_ref[PAYLOAD : PAYLOAD + 64, :])
    low = paired(wide_ref[PAYLOAD + 64 : WIDE, :])
    lane = lax.broadcasted_iota(jnp.int32, blocks.shape, 1)
    row = lax.broadcasted_iota(jnp.int32, blocks.shape, 0)
    second = lane >> 6
    region = blocks >> 3
    kblock = blocks & 7
    filled = jnp.where(region == 0, f_prev, jnp.where(region == 1, f_own, f_next))
    usable = (blocks >= 0) & (kblock * 128 + low < filled) & (base + row + 64 * second < f_own)
    place = jnp.where(region == 1, 0, jnp.where(region == 2 * odd, 2, 4)) + ((kblock & 1) ^ zh)
    target = jnp.where(usable, ((((kblock >> 1) - y) & 3) * 6 + place) * 8 + (row & 3) + 4 * second, -1)
    iota_p = lax.broadcasted_iota(jnp.int32, (192, 512), 0)
    iota_l = lax.broadcasted_iota(jnp.int32, (128, 512), 0)
    for i in range(16):
        line = lambda x: jnp.concatenate([x[4 * i + q : 4 * i + q + 1] for q in range(4)], axis=1)
        p = jnp.where(iota_p == line(target), 1.0, 0.0).astype(BF16)
        l = jnp.where(iota_l == line(low), 1.0, 0.0).astype(BF16)
        c = nt(p, l).reshape(24, 8, 128)
        for j, cnt_ref in enumerate((cnt0, cnt1, cnt2, cnt3)):
            cnt_ref[:, 4 * i : 4 * i + 4, :] = c[6 * j : 6 * j + 6, 0:4]
            cnt_ref[:, 64 + 4 * i : 68 + 4 * i, :] = c[6 * j : 6 * j + 6, 4:8]


def update(gathered, hidden, self_weight):
    drive = gathered * 0.125 + nn(hidden, self_weight)
    return (hidden.astype(F32) + drive * jax.nn.sigmoid(drive)).astype(BF16)


def mix(acc, mixing):
    total = acc[0:HALF] * mixing[0:1]
    for n in range(1, 8):
        total = total + acc[n * HALF : (n + 1) * HALF] * mixing[n : n + 1]
    return total


def rows_of(h, count):
    return pl.ds(pl.multiple_of(h * count, count), count)


def block_of(y_ref, c_ref, i):
    return y_ref[i] if i < 4 else c_ref[i - 4]


def here_of(near_ref, z, here_s):
    xyz = coordinates(near_ref[z])
    for d in range(3):
        here_s[d] = jnp.broadcast_to(xyz[d : d + 1], (128, ROWS)).T


def basis_half(h, shift_ref, y_ref, c_ref, cnt_ref, g_ref, here_s):
    for i in range(6):
        xyz = coordinates(block_of(y_ref, c_ref, i))
        x = xyz[0:1] + shift_ref[i // 2]
        for r in range(0, HALF, 32):
            rows = pl.ds(pl.multiple_of(h * HALF + r, 32), 32)
            dx = x - here_s[0, rows, :]
            dy = xyz[1:2] - here_s[1, rows, :]
            dz = xyz[2:3] - here_s[2, rows, :]
            v = dx * dx + dy * dy + dz * dz + (0.04 - CENTRE)
            cur = cnt_ref[i, rows, :] * horner(SINC, v)
            turn = horner(TWOCOS, v)
            prev = None
            for n in range(8):
                g_ref[pl.ds(pl.multiple_of(h * 512 + n * HALF + r, 32), 32), i * 128 : (i + 1) * 128] = cur.astype(BF16)
                if n < 7:
                    nxt = turn * cur if prev is None else turn * cur - prev
                    prev, cur = cur, nxt


def messages_of(y_ref, c_ref, weight):
    rows = jnp.concatenate([block_of(y_ref, c_ref, i)[0:ROWS, :] for i in range(6)], axis=0)
    return nn(rows, weight).astype(BF16)


def first_body(shift_ref, y_ref, c_ref, cnt_ref, edge_ref, mixing_ref, g_ref, part_ref, here_s, messages_s):
    messages_s[...] = messages_of(y_ref, c_ref, edge_ref[0])
    here_of(y_ref, 0, here_s)

    @pl.loop(0, 2)
    def _(h):
        basis_half(h, shift_ref, y_ref, c_ref, cnt_ref, g_ref, here_s)
        part_ref[rows_of(h, HALF), :] = mix(nn(g_ref[rows_of(h, 512), :], messages_s[...]), mixing_ref[0])


def first_rest_body(shift_ref, near_ref, y1, y2, y3, c1, c2, c3, n1, n2, n3, edge_ref, mixing_ref, part_ref, node_ref, g1, g2, g3, hidden_ref, here_s, messages_s, total_s):
    for j, (y, c) in enumerate(((y1, c1), (y2, c2), (y3, c3))):
        messages_s[j] = messages_of(y, c, edge_ref[0])
    here_of(near_ref, 0, here_s)

    @pl.loop(0, 2)
    def _(h):
        acc = None
        for j, (y, c, n, g) in enumerate(((y1, c1, n1, g1), (y2, c2, n2, g2), (y3, c3, n3, g3))):
            basis_half(h, shift_ref, y, c, n, g, here_s)
            term = nn(g[rows_of(h, 512), :], messages_s[j])
            acc = term if acc is None else acc + term
        total_s[rows_of(h, HALF), :] = mix(acc, mixing_ref[0])

    hidden_ref[...] = update(part_ref[...] + total_s[...], near_ref[0, 0:ROWS, :], node_ref[0])


def partner_body(shift_ref, near_ref, ya, yb, ca, cb, na, nb, ga, gb, here_s):
    here_of(near_ref, 1, here_s)

    @pl.loop(0, 2)
    def _(h):
        basis_half(h, shift_ref, ya, ca, na, ga, here_s)
        basis_half(h, shift_ref, yb, cb, nb, gb, here_s)


def second_body(y_ref, c_ref, own_ref, partner_ref, edge_ref, mixing_ref, part_ref, messages_s):
    messages_s[...] = messages_of(y_ref, c_ref, edge_ref[1])

    @pl.loop(0, 2)
    def _(h):
        for z, g in enumerate((own_ref, partner_ref)):
            part_ref[z, rows_of(h, HALF), :] = mix(nn(g[rows_of(h, 512), :], messages_s[...]), mixing_ref[1])


def second_rest_body(scal_ref, y1, y2, y3, c1, c2, c3, o1, o2, o3, p1, p2, p3, edge_ref, mixing_ref, part_ref, near_ref, node_ref, readout_ref, charge_ref, messages_s, total_s):
    for j, (y, c) in enumerate(((y1, c1), (y2, c2), (y3, c3))):
        messages_s[j] = messages_of(y, c, edge_ref[1])

    @pl.loop(0, 2)
    def _(h):
        for z, gs in enumerate(((o1, o2, o3), (p1, p2, p3))):
            acc = None
            for j, g in enumerate(gs):
                term = nn(g[rows_of(h, 512), :], messages_s[j])
                acc = term if acc is None else acc + term
            total_s[z, rows_of(h, HALF), :] = mix(acc, mixing_ref[1])

    for z in range(2):
        hidden = update(part_ref[z] + total_s[z], near_ref[z], node_ref[1])
        charges = nt(readout_ref[...], hidden)
        atom = lax.broadcasted_iota(jnp.int32, charges.shape, 1) + scal_ref[BASE + z]
        charge_ref[z] = jnp.where(atom < scal_ref[F_OWN], charges, 0.0)


def pair_body(in_ref, out_ref):
    out_ref[...] = in_ref[0:2]


def stack_body(a, b, c, d, out_ref):
    for i, ref in enumerate((a, b, c, d)):
        out_ref[i] = ref[0 : out_ref.shape[1], :]


def cross(pieces, left):
    hi, mid, lo = [p.astype(F32) for p in pieces]
    rows = [hi, hi, mid, hi, lo, mid] if left else [hi, mid, hi, lo, hi, mid]
    return jnp.concatenate(rows + [jnp.zeros((6, hi.shape[1]), F32)], axis=0)


def modes_body(modes_ref, out_ref):
    turns = modes_ref[...] * (0.5 / math.pi)
    out_ref[...] = cross(split(turns, 3), True).T.astype(BF16)


def phase_body(y_ref, modes_ref, wave_ref):

    @pl.loop(0, 2)
    def _(b):
        places = cross(split(coordinates(y_ref[b]), 3), False).astype(BF16)
        columns = pl.ds(pl.multiple_of(b * 128, 128), 128)
        for r in range(0, 1024, 64):
            turns = nn(modes_ref[r : r + 64, :], places)
            rest = turns - jnp.round(turns)
            square = rest * rest
            wave_ref[r : r + 64, columns] = horner(COSTURN, square).astype(BF16)
            wave_ref[r + 1024 : r + 1088, columns] = (rest * horner(SINTURN, square)).astype(BF16)


def structure_body(odd_ref, w0, w1, w2, w3, q0, q1, q2, q3, mine_ref, theirs_ref):
    pieces = [jnp.concatenate(split(jnp.concatenate([q[0], q[1]], axis=1), 3), axis=0) for q in (q0, q1, q2, q3)]
    odd = odd_ref[...] == 1
    for i in range(2):
        halves = []
        for r in (i * 1024, i * 1024 + 512):
            s = None
            for p, w in zip(pieces, (w0, w1, w2, w3)):
                term = nt(p, w[r : r + 512, :])
                s = term if s is None else s + term
            halves.append(s[0:16] + s[16:32] + s[32:48])
        mine_ref[16 * i : 16 * i + 16, :] = jnp.where(odd, halves[1], halves[0])
        theirs_ref[16 * i : 16 * i + 16, :] = jnp.where(odd, halves[0], halves[1])


def respond_body(scale, scal_ref, w0, w1, w2, w3, q0, q1, q2, q3, mine_ref, theirs_ref, modes_ref, out_ref):
    k = modes_ref[...]
    square = k[0:1] * k[0:1] + k[1:2] * k[1:2] + k[2:3] * k[2:3]
    weight = scale * jnp.exp(square * -0.125) / (square + 1.0)
    low = jnp.where(scal_ref[ODD] == 0, mine_ref[...], theirs_ref[...])
    high = jnp.where(scal_ref[ODD] == 0, theirs_ref[...], mine_ref[...])
    total = jnp.concatenate([low, high], axis=1) * weight
    real, imag = total[0:16], total[16:32]
    left = [real] + [imag * k[j : j + 1] for j in range(3)]
    right = [imag] + [real * -k[j : j + 1] for j in range(3)]
    both = jnp.concatenate([jnp.concatenate(left, axis=0), jnp.concatenate(right, axis=0)], axis=1)
    pieces = jnp.concatenate(split(both, 2), axis=0)
    for i, (w, q) in enumerate(zip((w0, w1, w2, w3), (q0, q1, q2, q3))):
        out = nn(pieces, w[...])
        out = out[0:64] + out[64:128]
        for b in range(2):
            mine = out[:, b * 128 : (b + 1) * 128]
            force = [-jnp.sum(mine[16 * j + 16 : 16 * j + 32] * q[b], axis=0, keepdims=True) for j in range(3)]
            out_ref[scal_ref[PLACE + 2 * i + b]] = jnp.concatenate([mine[0:16]] + force + [jnp.zeros((5, 128), F32)], axis=0)


def finish_body(parts_ref, potential_ref, forces_ref):
    total = parts_ref[0]
    for i in range(1, 8):
        total = total + parts_ref[i]
    potential_ref[...] = total[0:16]
    forces_ref[...] = total[16:19]


def pairs(n_slab, target):
    return [(s * 8 + k, (target(s, k)[0] % n_slab) * 8 + target(s, k)[1]) for s in range(n_slab) for k in range(8)]


def move(x, target):
    return lax.ppermute(x, AXES, pairs(lax.axis_size("slab"), target))


def over_chip(s):
    return s + 1 if s % 2 else s - 1


def near_blocks(block, wide):
    half = move(wide, lambda s, k: (s, k ^ 1))
    near = move(block, lambda s, k: (over_chip(s), k))
    both = move(block, lambda s, k: (over_chip(s), k ^ 1))
    return half, near, both


def along_y(block, near, name, after):
    stack = call(stack_body, jax.ShapeDtypeStruct((4,) + block.shape, BF16), block, *near, name=name, after=after)
    return [stack] + [move(stack, lambda s, k, j=j: (s, (k - 2 * j) % 8)) for j in range(1, 4)]


def other_core(y):
    return move(y[0:2], lambda s, k: (s ^ 1, k))


def other_core_after(y, name, after):
    pair = call(pair_body, jax.ShapeDtypeStruct((2,) + y.shape[1:], BF16), y, name=name, after=after)
    return move(pair, lambda s, k: (s ^ 1, k))


def shards(
    atom_descriptors,
    atom_locations,
    adjacent_atom_slots,
    neighbour_tally,
    filled_slot_tallies,
    reciprocal_lattice_modes,
    edge_update_matrix,
    node_update_matrix,
    distance_basis_mixing,
    latent_ionic_readout,
):
    n_slab = lax.axis_size("slab")
    shape = jax.ShapeDtypeStruct
    where = jnp.stack([lax.axis_index("slab"), lax.axis_index("kgrp")]).astype(jnp.int32)
    block, with_slots = call(
        pack_body, (shape((PAYLOAD, ROWS), BF16), shape((WIDE, ROWS), BF16)),
        atom_descriptors, atom_locations, adjacent_atom_slots.T, neighbour_tally.reshape(1, ROWS), name="pack",
    )
    near = near_blocks(block, with_slots)
    smem = pl.BlockSpec(memory_space=pltpu.SMEM)
    scal, shift, odd = call(
        layout_body, (shape((16,), jnp.int32), shape((3,), F32), shape((1, 512), jnp.int32)),
        scalars=(where, filled_slot_tallies), name="layout", out_specs=(smem, smem, pl.BlockSpec(memory_space=pltpu.VMEM)),
    )

    def count(source, which, name):
        return call(
            functools.partial(count_body, which), [shape((6, ROWS, 128), F32)] * 4, source, scalars=(scal,), name=name, flops=10**9
        )

    counts = count(with_slots, BASE, "counts")
    ys = along_y(block, near, "stack_first", (counts[0],))
    cs = [other_core(ys[0])]
    partner_counts = count(near[0], BASE_PARTNER, "partner_counts")
    wide = shape((8 * ROWS, 6 * ROWS), BF16)
    here = pltpu.VMEM((3, ROWS, 128), F32)
    message = lambda *n: pltpu.VMEM(n + (6 * ROWS, 128), BF16)
    basis = [None] * 4
    basis[0], part = call(
        first_body, (wide, shape((ROWS, 128), F32)),
        ys[0], cs[0], counts[0], edge_update_matrix, distance_basis_mixing,
        scalars=(shift,), name="first_0", flops=10**9, scratch=[here, message()],
    )
    cs += [other_core_after(ys[1], "pair_first", (part, partner_counts[0])), other_core(ys[2]), other_core(ys[3])]
    basis[1], basis[2], basis[3], hidden = call(
        first_rest_body, (wide, wide, wide, shape((ROWS, 128), BF16)),
        *ys, *cs[1:], *counts[1:], edge_update_matrix, distance_basis_mixing, part, node_update_matrix,
        scalars=(shift,), name="first_rest", flops=10**9, scratch=[here, message(3), pltpu.VMEM((ROWS, 128), F32)],
    )
    turns = call(modes_body, shape((1024, 24), BF16), reciprocal_lattice_modes, name="modes")

    def phases(j, after):
        return call(phase_body, shape((2048, 256), BF16), ys[j], turns, name=f"phases_{j}", flops=10**9, after=after)

    def partner_basis(a, b, after):
        return call(
            partner_body, [wide, wide], ys[0], ys[a], ys[b], cs[a], cs[b], partner_counts[a], partner_counts[b],
            scalars=(shift,), name=f"partner_{a}", flops=10**9, scratch=[here], after=after,
        )

    near = near_blocks(hidden, hidden)
    partner = [*partner_basis(0, 1, (hidden,))]
    waves = [phases(0, (hidden,))]
    ms = along_y(hidden, near, "stack_second", (partner[0], waves[0]))
    ns = [other_core(ms[0])]
    partner += [*partner_basis(2, 3, (ms[0],))]
    waves += [phases(1, (ms[0],))]
    part = call(
        second_body, shape((2, ROWS, 128), F32),
        ms[0], ns[0], basis[0], partner[0], edge_update_matrix, distance_basis_mixing,
        name="second_0", flops=10**9, scratch=[message()],
    )
    ns += [other_core_after(ms[1], "pair_second", (part, partner[2], *waves)), other_core(ms[2]), other_core(ms[3])]
    charges = call(
        second_rest_body, shape((2, 16, ROWS), F32),
        *ms[1:], *ns[1:], *basis[1:], *partner[1:], edge_update_matrix, distance_basis_mixing, part, ms[0], node_update_matrix, latent_ionic_readout.T,
        scalars=(scal,), name="second_rest", flops=10**9, scratch=[message(3), pltpu.VMEM((2, ROWS, 128), F32)],
    )
    qs = [charges] + [move(charges, lambda s, k, j=j: (s, (k - 2 * j) % 8)) for j in range(1, 4)]
    waves += [phases(j, (charges,)) for j in range(2, 4)]
    part, away = call(
        structure_body, (shape((32, 512), F32), shape((32, 512), F32)), odd, *waves, *qs,
        name="structure", flops=10**8,
    )
    part = part + move(away, lambda s, k: (s ^ 1, k))
    half = part.astype(BF16)
    part = part + sum(move(half, lambda s, k, m=m: (s + 8 * m, k)).astype(F32) for m in (1, 2, 3))
    half = part.astype(BF16)
    part = part + sum(move(half, lambda s, k, m=m: (s ^ (2 * m), k)).astype(F32) for m in (1, 2, 3))
    other = move(part, lambda s, k: (s ^ 1, k))
    scale = 4.0 / math.sqrt(n_slab * 1024 * reciprocal_lattice_modes.shape[1] * 8)
    partial = call(
        functools.partial(respond_body, scale), shape((8, 24, ROWS), F32), *waves, *qs, part, other, reciprocal_lattice_modes,
        scalars=(scal,), name="respond", flops=10**8,
    )
    partial = lax.all_to_all(partial, "kgrp", 0, 0)
    return tuple(call(finish_body, (shape((16, ROWS), F32), shape((3, ROWS), F32)), partial, name="finish"))


def solution(mesh):
    return jax.shard_map(
        shards,
        mesh=mesh,
        in_specs=(
            P(("slab", "kgrp"), None),
            P(None, ("slab", "kgrp")),
            P(("slab", "kgrp"), None),
            P(("slab", "kgrp")),
            P(),
            P(None, "kgrp"),
            P(),
            P(),
            P(),
            P(),
        ),
        out_specs=(P(None, ("slab", "kgrp")), P(None, ("slab", "kgrp"))),
        check_vma=False,
    )
```

```python
import functools
import math

import jax
import jax.numpy as jnp
from jax import lax
from jax.experimental import pallas as pl
from jax.experimental.pallas import tpu as pltpu
from jax.sharding import PartitionSpec as P

AXES = ("slab", "kgrp")
F32 = jnp.float32
BF16 = jnp.bfloat16
MIB = 1 << 20

ROWS = 128
PAYLOAD = 144
HALF = 64
WIDE = PAYLOAD + 128

Y, ZH, ODD, F_PREV, F_OWN, F_NEXT, BASE, BASE_PARTNER, PLACE = 0, 1, 2, 3, 4, 5, 6, 7, 8

CENTRE = 3.04
SINC = (0.4531433647, -0.11001027431, 0.0067080034928, -0.00018563842882, 2.9260279482e-06)
TWOCOS = (-0.504597100576, -0.581178942324, 0.0705470232447, -0.0028677843003, 5.9501086291e-05, -7.504320417652e-07)
SINTURN = (6.283184916495, -41.341589232689, 81.599943329776, -76.614472532619, 41.342882354378, -12.471243534759)
COSTURN = (0.99999921078, -19.738980355764, 64.92865742103, -85.271621534265, 58.790492119989, -21.071105627427)


def horner(coefficients, x):
    value = coefficients[-1] * x + coefficients[-2]
    for c in coefficients[-3::-1]:
        value = value * x + c
    return value


def split(x, parts):
    pieces = []
    for i in range(parts):
        piece = x.astype(BF16)
        pieces.append(piece)
        if i + 1 < parts:
            x = x - piece.astype(F32)
    return pieces


def nt(a, b):
    return lax.dot_general(a, b, (((1,), (1,)), ((), ())), preferred_element_type=F32)


def nn(a, b):
    return jnp.dot(a, b, preferred_element_type=F32)


def call(body, out_shape, *operands, scalars=(), after=(), name, flops=0, limit=12, scratch=(), **kw):
    n, m = len(scalars) + len(operands), len(after)
    return pl.pallas_call(
        lambda *refs: body(*refs[:n], *refs[n + m :]),
        out_shape=out_shape,
        in_specs=[pl.BlockSpec(memory_space=pltpu.SMEM)] * len(scalars)
        + [pl.BlockSpec(memory_space=pltpu.VMEM)] * len(operands)
        + [pl.BlockSpec(memory_space=pl.ANY)] * m,
        scratch_shapes=list(scratch),
        name=name,
        cost_estimate=pl.CostEstimate(flops=flops, bytes_accessed=MIB, transcendentals=0),
        compiler_params=pltpu.CompilerParams(vmem_limit_bytes=limit * MIB),
        **kw,
    )(*scalars, *operands, *after)


def pack_body(desc_ref, loc_ref, slots_ref, tally_ref, out_ref, wide_ref):
    hi, mid, lo = [p.astype(F32) for p in split(loc_ref[...], 3)]
    tail = jnp.concatenate([hi, mid, lo, jnp.zeros((7, ROWS), F32)], axis=0).astype(BF16)
    for ref in (out_ref, wide_ref):
        ref[0:ROWS, :] = desc_ref[...]
        ref[ROWS:PAYLOAD, :] = tail
    slots = slots_ref[...]
    used = lax.broadcasted_iota(jnp.int32, slots.shape, 0) < tally_ref[...]
    wide_ref[PAYLOAD : PAYLOAD + 64, :] = jnp.where(used, slots >> 7, -1).astype(F32).astype(BF16)
    wide_ref[PAYLOAD + 64 : WIDE, :] = (slots & 127).astype(F32).astype(BF16)


def layout_body(where_ref, filled_ref, scal_ref, shift_ref, odd_ref):
    slab, group = where_ref[0], where_ref[1]
    n_slab = filled_ref.shape[0]
    y, zh, odd = group >> 1, group & 1, slab & 1
    before = jnp.where(slab == 0, n_slab - 1, slab - 1)
    behind = jnp.where(slab == n_slab - 1, 0, slab + 1)
    scal_ref[Y] = y
    scal_ref[ZH] = zh
    scal_ref[ODD] = odd
    scal_ref[F_PREV] = filled_ref[before]
    scal_ref[F_OWN] = filled_ref[slab]
    scal_ref[F_NEXT] = filled_ref[behind]
    scal_ref[BASE] = group * ROWS
    scal_ref[BASE_PARTNER] = (group ^ 1) * ROWS
    for i in range(8):
        scal_ref[PLACE + i] = (((y + i // 2) & 3) << 1) | ((i % 2) ^ zh)
    low_edge = jnp.where(slab == 0, -float(n_slab), 0.0)
    high_edge = jnp.where(slab == n_slab - 1, float(n_slab), 0.0)
    shift_ref[0] = 0.0
    shift_ref[1] = jnp.where(odd == 1, high_edge, low_edge)
    shift_ref[2] = jnp.where(odd == 1, low_edge, high_edge)
    odd_ref[...] = jnp.full((1, 512), odd, jnp.int32)


def coordinates(payload):
    tail = payload[ROWS:PAYLOAD, :].astype(F32)
    return (tail[0:3] + tail[3:6]) + tail[6:9]


def count_body(which, scal_ref, wide_ref, cnt0, cnt1, cnt2, cnt3):
    y, zh, odd = scal_ref[Y], scal_ref[ZH], scal_ref[ODD]
    f_prev, f_own, f_next, base = scal_ref[F_PREV], scal_ref[F_OWN], scal_ref[F_NEXT], scal_ref[which]

    def paired(rows):
        t = rows.astype(F32).T
        return jnp.concatenate([t[0:64], t[64:128]], axis=1).astype(jnp.int32)

    blocks = paired(wide_ref[PAYLOAD : PAYLOAD + 64, :])
    low = paired(wide_ref[PAYLOAD + 64 : WIDE, :])
    lane = lax.broadcasted_iota(jnp.int32, blocks.shape, 1)
    row = lax.broadcasted_iota(jnp.int32, blocks.shape, 0)
    second = lane >> 6
    region = blocks >> 3
    kblock = blocks & 7
    filled = jnp.where(region == 0, f_prev, jnp.where(region == 1, f_own, f_next))
    usable = (blocks >= 0) & (kblock * 128 + low < filled) & (base + row + 64 * second < f_own)
    place = jnp.where(region == 1, 0, jnp.where(region == 2 * odd, 2, 4)) + ((kblock & 1) ^ zh)
    target = jnp.where(usable, ((((kblock >> 1) - y) & 3) * 6 + place) * 8 + (row & 3) + 4 * second, -1)
    iota_p = lax.broadcasted_iota(jnp.int32, (192, 512), 0)
    iota_l = lax.broadcasted_iota(jnp.int32, (128, 512), 0)
    for i in range(16):
        line = lambda x: jnp.concatenate([x[4 * i + q : 4 * i + q + 1] for q in range(4)], axis=1)
        p = jnp.where(iota_p == line(target), 1.0, 0.0).astype(BF16)
        l = jnp.where(iota_l == line(low), 1.0, 0.0).astype(BF16)
        c = nt(p, l).reshape(24, 8, 128)
        for j, cnt_ref in enumerate((cnt0, cnt1, cnt2, cnt3)):
            cnt_ref[:, 4 * i : 4 * i + 4, :] = c[6 * j : 6 * j + 6, 0:4]
            cnt_ref[:, 64 + 4 * i : 68 + 4 * i, :] = c[6 * j : 6 * j + 6, 4:8]


def update(gathered, hidden, self_weight):
    drive = gathered * 0.125 + nn(hidden, self_weight)
    return (hidden.astype(F32) + drive * jax.nn.sigmoid(drive)).astype(BF16)


def mix(acc, mixing):
    total = acc[0:HALF] * mixing[0:1]
    for n in range(1, 8):
        total = total + acc[n * HALF : (n + 1) * HALF] * mixing[n : n + 1]
    return total


def aligned(start):
    return pl.ds(start if isinstance(start, int) else pl.multiple_of(start, 32), 32)


def rows_of(h, count):
    if isinstance(h, int):
        return pl.ds(h * count, count)
    return pl.ds(pl.multiple_of(h * count, count), count)


def block_of(y_ref, c_ref, i):
    return y_ref[i] if i < 4 else c_ref[i - 4]


def here_of(near_ref, z, here_s):
    xyz = coordinates(near_ref[z])
    for d in range(3):
        here_s[d] = jnp.broadcast_to(xyz[d : d + 1], (128, ROWS)).T


def basis_half(h, shift_ref, y_ref, c_ref, cnt_ref, g_ref, here_s):
    for i in range(6):
        xyz = coordinates(block_of(y_ref, c_ref, i))
        x = xyz[0:1] + shift_ref[i // 2]
        for r in range(0, HALF, 32):
            rows = aligned(h * HALF + r)
            dx = x - here_s[0, rows, :]
            dy = xyz[1:2] - here_s[1, rows, :]
            dz = xyz[2:3] - here_s[2, rows, :]
            v = dx * dx + dy * dy + dz * dz + (0.04 - CENTRE)
            cur = cnt_ref[i, rows, :] * horner(SINC, v)
            turn = horner(TWOCOS, v)
            prev = None
            for n in range(8):
                g_ref[aligned(h * 512 + n * HALF + r), i * 128 : (i + 1) * 128] = cur.astype(BF16)
                if n < 7:
                    nxt = turn * cur if prev is None else turn * cur - prev
                    prev, cur = cur, nxt


def messages_of(y_ref, c_ref, weight):
    rows = jnp.concatenate([block_of(y_ref, c_ref, i)[0:ROWS, :] for i in range(6)], axis=0)
    return nn(rows, weight).astype(BF16)


def first_body(shift_ref, y_ref, c_ref, cnt_ref, edge_ref, mixing_ref, g_ref, part_ref, here_s, messages_s):
    messages_s[...] = messages_of(y_ref, c_ref, edge_ref[0])
    here_of(y_ref, 0, here_s)

    @pl.loop(0, 2)
    def _(h):
        basis_half(h, shift_ref, y_ref, c_ref, cnt_ref, g_ref, here_s)
        part_ref[rows_of(h, HALF), :] = mix(nn(g_ref[rows_of(h, 512), :], messages_s[...]), mixing_ref[0])


def first_rest_body(shift_ref, near_ref, y1, y2, y3, c1, c2, c3, n1, n2, n3, edge_ref, mixing_ref, part_ref, node_ref, g1, g2, g3, hidden_ref, here_s, messages_s, total_s):
    for j, (y, c) in enumerate(((y1, c1), (y2, c2), (y3, c3))):
        messages_s[j] = messages_of(y, c, edge_ref[0])
    here_of(near_ref, 0, here_s)

    for h in range(2):
        acc = None
        for j, (y, c, n, g) in enumerate(((y1, c1, n1, g1), (y2, c2, n2, g2), (y3, c3, n3, g3))):
            basis_half(h, shift_ref, y, c, n, g, here_s)
            term = nn(g[rows_of(h, 512), :], messages_s[j])
            acc = term if acc is None else acc + term
        total_s[rows_of(h, HALF), :] = mix(acc, mixing_ref[0])

    hidden_ref[...] = update(part_ref[...] + total_s[...], near_ref[0, 0:ROWS, :], node_ref[0])


def partner_body(shift_ref, near_ref, ya, yb, ca, cb, na, nb, ga, gb, here_s):
    here_of(near_ref, 1, here_s)

    @pl.loop(0, 2)
    def _(h):
        basis_half(h, shift_ref, ya, ca, na, ga, here_s)
        basis_half(h, shift_ref, yb, cb, nb, gb, here_s)


def second_body(y_ref, c_ref, own_ref, partner_ref, edge_ref, mixing_ref, part_ref, messages_s):
    messages_s[...] = messages_of(y_ref, c_ref, edge_ref[1])

    for h in range(2):
        for z, g in enumerate((own_ref, partner_ref)):
            part_ref[z, rows_of(h, HALF), :] = mix(nn(g[rows_of(h, 512), :], messages_s[...]), mixing_ref[1])


def second_rest_body(scal_ref, y1, y2, y3, c1, c2, c3, o1, o2, o3, p1, p2, p3, edge_ref, mixing_ref, part_ref, near_ref, node_ref, readout_ref, charge_ref, messages_s, total_s):
    for j, (y, c) in enumerate(((y1, c1), (y2, c2), (y3, c3))):
        messages_s[j] = messages_of(y, c, edge_ref[1])

    for h in range(2):
        for z, gs in enumerate(((o1, o2, o3), (p1, p2, p3))):
            acc = None
            for j, g in enumerate(gs):
                term = nn(g[rows_of(h, 512), :], messages_s[j])
                acc = term if acc is None else acc + term
            total_s[z, rows_of(h, HALF), :] = mix(acc, mixing_ref[1])

    for z in range(2):
        hidden = update(part_ref[z] + total_s[z], near_ref[z], node_ref[1])
        charges = nt(readout_ref[...], hidden)
        atom = lax.broadcasted_iota(jnp.int32, charges.shape, 1) + scal_ref[BASE + z]
        charge_ref[z] = jnp.where(atom < scal_ref[F_OWN], charges, 0.0)


def pair_body(in_ref, out_ref):
    out_ref[...] = in_ref[0:2]


def stack_body(a, b, c, d, out_ref):
    for i, ref in enumerate((a, b, c, d)):
        out_ref[i] = ref[0 : out_ref.shape[1], :]


def cross(pieces, left):
    hi, mid, lo = [p.astype(F32) for p in pieces]
    rows = [hi, hi, mid, hi, lo, mid] if left else [hi, mid, hi, lo, hi, mid]
    return jnp.concatenate(rows + [jnp.zeros((6, hi.shape[1]), F32)], axis=0)


def modes_body(modes_ref, out_ref):
    turns = modes_ref[...] * (0.5 / math.pi)
    out_ref[...] = cross(split(turns, 3), True).T.astype(BF16)


def phase_body(y_ref, modes_ref, wave_ref):

    @pl.loop(0, 2)
    def _(b):
        places = cross(split(coordinates(y_ref[b]), 3), False).astype(BF16)
        columns = pl.ds(pl.multiple_of(b * 128, 128), 128)
        for r in range(0, 1024, 64):
            turns = nn(modes_ref[r : r + 64, :], places)
            rest = turns - jnp.round(turns)
            square = rest * rest
            wave_ref[r : r + 64, columns] = horner(COSTURN, square).astype(BF16)
            wave_ref[r + 1024 : r + 1088, columns] = (rest * horner(SINTURN, square)).astype(BF16)


def structure_body(odd_ref, w0, w1, w2, w3, q0, q1, q2, q3, mine_ref, theirs_ref):
    pieces = [jnp.concatenate(split(jnp.concatenate([q[0], q[1]], axis=1), 3), axis=0) for q in (q0, q1, q2, q3)]
    odd = odd_ref[...] == 1
    for i in range(2):
        halves = []
        for r in (i * 1024, i * 1024 + 512):
            s = None
            for p, w in zip(pieces, (w0, w1, w2, w3)):
                term = nt(p, w[r : r + 512, :])
                s = term if s is None else s + term
            halves.append(s[0:16] + s[16:32] + s[32:48])
        mine_ref[16 * i : 16 * i + 16, :] = jnp.where(odd, halves[1], halves[0])
        theirs_ref[16 * i : 16 * i + 16, :] = jnp.where(odd, halves[0], halves[1])


def respond_body(scale, scal_ref, w0, w1, w2, w3, q0, q1, q2, q3, mine_ref, theirs_ref, modes_ref, out_ref):
    k = modes_ref[...]
    square = k[0:1] * k[0:1] + k[1:2] * k[1:2] + k[2:3] * k[2:3]
    weight = scale * jnp.exp(square * -0.125) / (square + 1.0)
    low = jnp.where(scal_ref[ODD] == 0, mine_ref[...], theirs_ref[...])
    high = jnp.where(scal_ref[ODD] == 0, theirs_ref[...], mine_ref[...])
    total = jnp.concatenate([low, high], axis=1) * weight
    real, imag = total[0:16], total[16:32]
    left = [real] + [imag * k[j : j + 1] for j in range(3)]
    right = [imag] + [real * -k[j : j + 1] for j in range(3)]
    both = jnp.concatenate([jnp.concatenate(left, axis=0), jnp.concatenate(right, axis=0)], axis=1)
    pieces = jnp.concatenate(split(both, 2), axis=0)
    for i, (w, q) in enumerate(zip((w0, w1, w2, w3), (q0, q1, q2, q3))):
        out = nn(pieces, w[...])
        out = out[0:64] + out[64:128]
        for b in range(2):
            mine = out[:, b * 128 : (b + 1) * 128]
            force = [-jnp.sum(mine[16 * j + 16 : 16 * j + 32] * q[b], axis=0, keepdims=True) for j in range(3)]
            out_ref[scal_ref[PLACE + 2 * i + b]] = jnp.concatenate([mine[0:16]] + force + [jnp.zeros((5, 128), F32)], axis=0)


def finish_body(parts_ref, potential_ref, forces_ref):
    total = parts_ref[0]
    for i in range(1, 8):
        total = total + parts_ref[i]
    potential_ref[...] = total[0:16]
    forces_ref[...] = total[16:19]


def pairs(n_slab, target):
    return [(s * 8 + k, (target(s, k)[0] % n_slab) * 8 + target(s, k)[1]) for s in range(n_slab) for k in range(8)]


def move(x, target):
    return lax.ppermute(x, AXES, pairs(lax.axis_size("slab"), target))


def over_chip(s):
    return s + 1 if s % 2 else s - 1


def near_blocks(block, wide):
    half = move(wide, lambda s, k: (s, k ^ 1))
    near = move(block, lambda s, k: (over_chip(s), k))
    both = move(block, lambda s, k: (over_chip(s), k ^ 1))
    return half, near, both


def along_y(block, near, name, after):
    stack = call(stack_body, jax.ShapeDtypeStruct((4,) + block.shape, BF16), block, *near, name=name, after=after)
    return [stack] + [move(stack, lambda s, k, j=j: (s, (k - 2 * j) % 8)) for j in range(1, 4)]


def other_core(y):
    return move(y[0:2], lambda s, k: (s ^ 1, k))


def other_core_after(y, name, after):
    pair = call(pair_body, jax.ShapeDtypeStruct((2,) + y.shape[1:], BF16), y, name=name, after=after)
    return move(pair, lambda s, k: (s ^ 1, k))


def shards(
    atom_descriptors,
    atom_locations,
    adjacent_atom_slots,
    neighbour_tally,
    filled_slot_tallies,
    reciprocal_lattice_modes,
    edge_update_matrix,
    node_update_matrix,
    distance_basis_mixing,
    latent_ionic_readout,
):
    n_slab = lax.axis_size("slab")
    shape = jax.ShapeDtypeStruct
    where = jnp.stack([lax.axis_index("slab"), lax.axis_index("kgrp")]).astype(jnp.int32)
    block, with_slots = call(
        pack_body, (shape((PAYLOAD, ROWS), BF16), shape((WIDE, ROWS), BF16)),
        atom_descriptors, atom_locations, adjacent_atom_slots.T, neighbour_tally.reshape(1, ROWS), name="pack", limit=56,
    )
    near = near_blocks(block, with_slots)
    smem = pl.BlockSpec(memory_space=pltpu.SMEM)
    scal, shift, odd = call(
        layout_body, (shape((16,), jnp.int32), shape((3,), F32), shape((1, 512), jnp.int32)),
        scalars=(where, filled_slot_tallies), name="layout", out_specs=(smem, smem, pl.BlockSpec(memory_space=pltpu.VMEM)),
    )

    def count(source, which, name):
        return call(
            functools.partial(count_body, which), [shape((6, ROWS, 128), F32)] * 4, source, scalars=(scal,), name=name, flops=10**9
        )

    counts = count(with_slots, BASE, "counts")
    ys = along_y(block, near, "stack_first", (counts[0],))
    cs = [other_core(ys[0])]
    partner_counts = count(near[0], BASE_PARTNER, "partner_counts")
    wide = shape((8 * ROWS, 6 * ROWS), BF16)
    here = pltpu.VMEM((3, ROWS, 128), F32)
    message = lambda *n: pltpu.VMEM(n + (6 * ROWS, 128), BF16)
    basis = [None] * 4
    basis[0], part = call(
        first_body, (wide, shape((ROWS, 128), F32)),
        ys[0], cs[0], counts[0], edge_update_matrix, distance_basis_mixing,
        scalars=(shift,), name="first_0", flops=10**9, scratch=[here, message()],
    )
    cs += [other_core_after(ys[1], "pair_first", (part, partner_counts[0])), other_core(ys[2]), other_core(ys[3])]
    basis[1], basis[2], basis[3], hidden = call(
        first_rest_body, (wide, wide, wide, shape((ROWS, 128), BF16)),
        *ys, *cs[1:], *counts[1:], edge_update_matrix, distance_basis_mixing, part, node_update_matrix,
        scalars=(shift,), name="first_rest", flops=10**9, scratch=[here, message(3), pltpu.VMEM((ROWS, 128), F32)],
    )
    turns = call(modes_body, shape((1024, 24), BF16), reciprocal_lattice_modes, name="modes")

    def phases(j, after):
        return call(phase_body, shape((2048, 256), BF16), ys[j], turns, name=f"phases_{j}", flops=10**9, after=after)

    def partner_basis(a, b, after):
        return call(
            partner_body, [wide, wide], ys[0], ys[a], ys[b], cs[a], cs[b], partner_counts[a], partner_counts[b],
            scalars=(shift,), name=f"partner_{a}", flops=10**9, scratch=[here], after=after,
        )

    near = near_blocks(hidden, hidden)
    partner = [*partner_basis(0, 1, (hidden,))]
    waves = [phases(0, (hidden,))]
    ms = along_y(hidden, near, "stack_second", (partner[0], waves[0]))
    ns = [other_core(ms[0])]
    partner += [*partner_basis(2, 3, (ms[0],))]
    waves += [phases(1, (ms[0],))]
    part = call(
        second_body, shape((2, ROWS, 128), F32),
        ms[0], ns[0], basis[0], partner[0], edge_update_matrix, distance_basis_mixing,
        name="second_0", flops=10**9, scratch=[message()],
    )
    ns += [other_core_after(ms[1], "pair_second", (part, partner[2], *waves)), other_core(ms[2]), other_core(ms[3])]
    charges = call(
        second_rest_body, shape((2, 16, ROWS), F32),
        *ms[1:], *ns[1:], *basis[1:], *partner[1:], edge_update_matrix, distance_basis_mixing, part, ms[0], node_update_matrix, latent_ionic_readout.T,
        scalars=(scal,), name="second_rest", flops=10**9, scratch=[message(3), pltpu.VMEM((2, ROWS, 128), F32)],
    )
    qs = [charges] + [move(charges, lambda s, k, j=j: (s, (k - 2 * j) % 8)) for j in range(1, 4)]
    waves += [phases(j, (charges,)) for j in range(2, 4)]
    part, away = call(
        structure_body, (shape((32, 512), F32), shape((32, 512), F32)), odd, *waves, *qs,
        name="structure", flops=10**8,
    )
    part = part + move(away, lambda s, k: (s ^ 1, k))
    half = part.astype(BF16)
    part = part + sum(move(half, lambda s, k, m=m: (s + 8 * m, k)).astype(F32) for m in (1, 2, 3))
    half = part.astype(BF16)
    part = part + sum(move(half, lambda s, k, m=m: (s ^ (2 * m), k)).astype(F32) for m in (1, 2, 3))
    other = move(part, lambda s, k: (s ^ 1, k))
    scale = 4.0 / math.sqrt(n_slab * 1024 * reciprocal_lattice_modes.shape[1] * 8)
    partial = call(
        functools.partial(respond_body, scale), shape((8, 24, ROWS), F32), *waves, *qs, part, other, reciprocal_lattice_modes,
        scalars=(scal,), name="respond", flops=10**8,
    )
    partial = lax.all_to_all(partial, "kgrp", 0, 0)
    return tuple(call(finish_body, (shape((16, ROWS), F32), shape((3, ROWS), F32)), partial, name="finish"))


def solution(mesh):
    return jax.shard_map(
        shards,
        mesh=mesh,
        in_specs=(
            P(("slab", "kgrp"), None),
            P(None, ("slab", "kgrp")),
            P(("slab", "kgrp"), None),
            P(("slab", "kgrp")),
            P(),
            P(None, "kgrp"),
            P(),
            P(),
            P(),
            P(),
        ),
        out_specs=(P(None, ("slab", "kgrp")), P(None, ("slab", "kgrp"))),
        check_vma=False,
    )
```

```python
import functools
import math

import jax
import jax.numpy as jnp
from jax import lax
from jax.experimental import pallas as pl
from jax.experimental.pallas import tpu as pltpu
from jax.sharding import PartitionSpec as P

AXES = ("slab", "kgrp")
F32 = jnp.float32
BF16 = jnp.bfloat16
MIB = 1 << 20

ROWS = 128
PAYLOAD = 144
HALF = 64
WIDE = PAYLOAD + 128

Y, ZH, ODD, F_PREV, F_OWN, F_NEXT, BASE, BASE_PARTNER, PLACE = 0, 1, 2, 3, 4, 5, 6, 7, 8

CENTRE = 3.04
SINC = (0.4531433647, -0.11001027431, 0.0067080034928, -0.00018563842882, 2.9260279482e-06)
TWOCOS = (-0.504597100576, -0.581178942324, 0.0705470232447, -0.0028677843003, 5.9501086291e-05, -7.504320417652e-07)
SINTURN = (6.283184916495, -41.341589232689, 81.599943329776, -76.614472532619, 41.342882354378, -12.471243534759)
COSTURN = (0.99999921078, -19.738980355764, 64.92865742103, -85.271621534265, 58.790492119989, -21.071105627427)


def horner(coefficients, x):
    value = coefficients[-1] * x + coefficients[-2]
    for c in coefficients[-3::-1]:
        value = value * x + c
    return value


def split(x, parts):
    pieces = []
    for i in range(parts):
        piece = x.astype(BF16)
        pieces.append(piece)
        if i + 1 < parts:
            x = x - piece.astype(F32)
    return pieces


def nt(a, b):
    return lax.dot_general(a, b, (((1,), (1,)), ((), ())), preferred_element_type=F32)


def nn(a, b):
    return jnp.dot(a, b, preferred_element_type=F32)


def call(body, out_shape, *operands, scalars=(), after=(), name, flops=0, limit=12, scratch=(), **kw):
    n, m = len(scalars) + len(operands), len(after)
    return pl.pallas_call(
        lambda *refs: body(*refs[:n], *refs[n + m :]),
        out_shape=out_shape,
        in_specs=[pl.BlockSpec(memory_space=pltpu.SMEM)] * len(scalars)
        + [pl.BlockSpec(memory_space=pltpu.VMEM)] * len(operands)
        + [pl.BlockSpec(memory_space=pl.ANY)] * m,
        scratch_shapes=list(scratch),
        name=name,
        cost_estimate=pl.CostEstimate(flops=flops, bytes_accessed=MIB, transcendentals=0),
        compiler_params=pltpu.CompilerParams(vmem_limit_bytes=limit * MIB),
        **kw,
    )(*scalars, *operands, *after)


def pack_body(desc_ref, loc_ref, slots_ref, tally_ref, out_ref, wide_ref):
    hi, mid, lo = [p.astype(F32) for p in split(loc_ref[...], 3)]
    tail = jnp.concatenate([hi, mid, lo, jnp.zeros((7, ROWS), F32)], axis=0).astype(BF16)
    for ref in (out_ref, wide_ref):
        ref[0:ROWS, :] = desc_ref[...]
        ref[ROWS:PAYLOAD, :] = tail
    slots = slots_ref[...]
    used = lax.broadcasted_iota(jnp.int32, slots.shape, 0) < tally_ref[...]
    wide_ref[PAYLOAD : PAYLOAD + 64, :] = jnp.where(used, slots >> 7, -1).astype(F32).astype(BF16)
    wide_ref[PAYLOAD + 64 : WIDE, :] = (slots & 127).astype(F32).astype(BF16)


def layout_body(where_ref, filled_ref, scal_ref, shift_ref, odd_ref):
    slab, group = where_ref[0], where_ref[1]
    n_slab = filled_ref.shape[0]
    y, zh, odd = group >> 1, group & 1, slab & 1
    before = jnp.where(slab == 0, n_slab - 1, slab - 1)
    behind = jnp.where(slab == n_slab - 1, 0, slab + 1)
    scal_ref[Y] = y
    scal_ref[ZH] = zh
    scal_ref[ODD] = odd
    scal_ref[F_PREV] = filled_ref[before]
    scal_ref[F_OWN] = filled_ref[slab]
    scal_ref[F_NEXT] = filled_ref[behind]
    scal_ref[BASE] = group * ROWS
    scal_ref[BASE_PARTNER] = (group ^ 1) * ROWS
    for i in range(8):
        scal_ref[PLACE + i] = (((y + i // 2) & 3) << 1) | ((i % 2) ^ zh)
    low_edge = jnp.where(slab == 0, -float(n_slab), 0.0)
    high_edge = jnp.where(slab == n_slab - 1, float(n_slab), 0.0)
    shift_ref[0] = 0.0
    shift_ref[1] = jnp.where(odd == 1, high_edge, low_edge)
    shift_ref[2] = jnp.where(odd == 1, low_edge, high_edge)
    odd_ref[...] = jnp.full((1, 512), odd, jnp.int32)


def coordinates(payload):
    tail = payload[ROWS:PAYLOAD, :].astype(F32)
    return (tail[0:3] + tail[3:6]) + tail[6:9]


def count_body(which, scal_ref, wide_ref, cnt0, cnt1, cnt2, cnt3):
    y, zh, odd = scal_ref[Y], scal_ref[ZH], scal_ref[ODD]
    f_prev, f_own, f_next, base = scal_ref[F_PREV], scal_ref[F_OWN], scal_ref[F_NEXT], scal_ref[which]

    def paired(rows):
        t = rows.astype(F32).T
        return jnp.concatenate([t[0:64], t[64:128]], axis=1).astype(jnp.int32)

    blocks = paired(wide_ref[PAYLOAD : PAYLOAD + 64, :])
    low = paired(wide_ref[PAYLOAD + 64 : WIDE, :])
    lane = lax.broadcasted_iota(jnp.int32, blocks.shape, 1)
    row = lax.broadcasted_iota(jnp.int32, blocks.shape, 0)
    second = lane >> 6
    region = blocks >> 3
    kblock = blocks & 7
    filled = jnp.where(region == 0, f_prev, jnp.where(region == 1, f_own, f_next))
    usable = (blocks >= 0) & (kblock * 128 + low < filled) & (base + row + 64 * second < f_own)
    place = jnp.where(region == 1, 0, jnp.where(region == 2 * odd, 2, 4)) + ((kblock & 1) ^ zh)
    target = jnp.where(usable, ((((kblock >> 1) - y) & 3) * 6 + place) * 8 + (row & 3) + 4 * second, -1)
    iota_p = lax.broadcasted_iota(jnp.int32, (192, 512), 0)
    iota_l = lax.broadcasted_iota(jnp.int32, (128, 512), 0)
    for i in range(16):
        line = lambda x: jnp.concatenate([x[4 * i + q : 4 * i + q + 1] for q in range(4)], axis=1)
        p = jnp.where(iota_p == line(target), 1.0, 0.0).astype(BF16)
        l = jnp.where(iota_l == line(low), 1.0, 0.0).astype(BF16)
        c = nt(p, l).reshape(24, 8, 128)
        for j, cnt_ref in enumerate((cnt0, cnt1, cnt2, cnt3)):
            cnt_ref[:, 4 * i : 4 * i + 4, :] = c[6 * j : 6 * j + 6, 0:4]
            cnt_ref[:, 64 + 4 * i : 68 + 4 * i, :] = c[6 * j : 6 * j + 6, 4:8]


def update(gathered, hidden, self_weight):
    drive = gathered * 0.125 + nn(hidden, self_weight)
    return (hidden.astype(F32) + drive * jax.nn.sigmoid(drive)).astype(BF16)


def mix(acc, mixing):
    total = acc[0:HALF] * mixing[0:1]
    for n in range(1, 8):
        total = total + acc[n * HALF : (n + 1) * HALF] * mixing[n : n + 1]
    return total


def aligned(start):
    return pl.ds(start if isinstance(start, int) else pl.multiple_of(start, 32), 32)


def rows_of(h, count):
    if isinstance(h, int):
        return pl.ds(h * count, count)
    return pl.ds(pl.multiple_of(h * count, count), count)


def block_of(y_ref, c_ref, i):
    return y_ref[i] if i < 4 else c_ref[i - 4]


def here_of(near_ref, z, here_s):
    xyz = coordinates(near_ref[z])
    for d in range(3):
        here_s[d] = jnp.broadcast_to(xyz[d : d + 1], (128, ROWS)).T


def basis_half(h, shift_ref, y_ref, c_ref, cnt_ref, g_ref, here_s):
    for i in range(6):
        xyz = coordinates(block_of(y_ref, c_ref, i))
        x = xyz[0:1] + shift_ref[i // 2]
        for r in range(0, HALF, 32):
            rows = aligned(h * HALF + r)
            dx = x - here_s[0, rows, :]
            dy = xyz[1:2] - here_s[1, rows, :]
            dz = xyz[2:3] - here_s[2, rows, :]
            v = dx * dx + dy * dy + dz * dz + (0.04 - CENTRE)
            cur = cnt_ref[i, rows, :] * horner(SINC, v)
            turn = horner(TWOCOS, v)
            prev = None
            for n in range(8):
                g_ref[aligned(h * 512 + n * HALF + r), i * 128 : (i + 1) * 128] = cur.astype(BF16)
                if n < 7:
                    nxt = turn * cur if prev is None else turn * cur - prev
                    prev, cur = cur, nxt


def messages_of(y_ref, c_ref, weight):
    rows = jnp.concatenate([block_of(y_ref, c_ref, i)[0:ROWS, :] for i in range(6)], axis=0)
    return nn(rows, weight).astype(BF16)


def first_body(shift_ref, y_ref, c_ref, cnt_ref, edge_ref, mixing_ref, g_ref, part_ref, here_s, messages_s):
    messages_s[...] = messages_of(y_ref, c_ref, edge_ref[0])
    here_of(y_ref, 0, here_s)

    @pl.loop(0, 2)
    def _(h):
        basis_half(h, shift_ref, y_ref, c_ref, cnt_ref, g_ref, here_s)
        part_ref[rows_of(h, HALF), :] = mix(nn(g_ref[rows_of(h, 512), :], messages_s[...]), mixing_ref[0])


def first_rest_body(shift_ref, near_ref, y1, y2, y3, c1, c2, c3, n1, n2, n3, edge_ref, mixing_ref, part_ref, node_ref, g1, g2, g3, hidden_ref, here_s, messages_s, total_s):
    for j, (y, c) in enumerate(((y1, c1), (y2, c2), (y3, c3))):
        messages_s[j] = messages_of(y, c, edge_ref[0])
    here_of(near_ref, 0, here_s)

    for h in range(2):
        acc = None
        for j, (y, c, n, g) in enumerate(((y1, c1, n1, g1), (y2, c2, n2, g2), (y3, c3, n3, g3))):
            basis_half(h, shift_ref, y, c, n, g, here_s)
            term = nn(g[rows_of(h, 512), :], messages_s[j])
            acc = term if acc is None else acc + term
        total_s[rows_of(h, HALF), :] = mix(acc, mixing_ref[0])

    hidden_ref[...] = update(part_ref[...] + total_s[...], near_ref[0, 0:ROWS, :], node_ref[0])


def partner_body(shift_ref, near_ref, ya, yb, ca, cb, na, nb, ga, gb, here_s):
    here_of(near_ref, 1, here_s)

    for h in range(2):
        basis_half(h, shift_ref, ya, ca, na, ga, here_s)
        basis_half(h, shift_ref, yb, cb, nb, gb, here_s)


def second_body(y_ref, c_ref, own_ref, partner_ref, edge_ref, mixing_ref, part_ref, messages_s):
    messages_s[...] = messages_of(y_ref, c_ref, edge_ref[1])

    for h in range(2):
        for z, g in enumerate((own_ref, partner_ref)):
            part_ref[z, rows_of(h, HALF), :] = mix(nn(g[rows_of(h, 512), :], messages_s[...]), mixing_ref[1])


def second_rest_body(scal_ref, y1, y2, y3, c1, c2, c3, o1, o2, o3, p1, p2, p3, edge_ref, mixing_ref, part_ref, near_ref, node_ref, readout_ref, charge_ref, messages_s, total_s):
    for j, (y, c) in enumerate(((y1, c1), (y2, c2), (y3, c3))):
        messages_s[j] = messages_of(y, c, edge_ref[1])

    for h in range(2):
        for z, gs in enumerate(((o1, o2, o3), (p1, p2, p3))):
            acc = None
            for j, g in enumerate(gs):
                term = nn(g[rows_of(h, 512), :], messages_s[j])
                acc = term if acc is None else acc + term
            total_s[z, rows_of(h, HALF), :] = mix(acc, mixing_ref[1])

    for z in range(2):
        hidden = update(part_ref[z] + total_s[z], near_ref[z], node_ref[1])
        charges = nt(readout_ref[...], hidden)
        atom = lax.broadcasted_iota(jnp.int32, charges.shape, 1) + scal_ref[BASE + z]
        charge_ref[z] = jnp.where(atom < scal_ref[F_OWN], charges, 0.0)


def pair_body(in_ref, out_ref):
    out_ref[...] = in_ref[0:2]


def stack_body(a, b, c, d, out_ref):
    for i, ref in enumerate((a, b, c, d)):
        out_ref[i] = ref[0 : out_ref.shape[1], :]


def cross(pieces, left):
    hi, mid, lo = [p.astype(F32) for p in pieces]
    rows = [hi, hi, mid, hi, lo, mid] if left else [hi, mid, hi, lo, hi, mid]
    return jnp.concatenate(rows + [jnp.zeros((6, hi.shape[1]), F32)], axis=0)


def modes_body(modes_ref, out_ref):
    turns = modes_ref[...] * (0.5 / math.pi)
    out_ref[...] = cross(split(turns, 3), True).T.astype(BF16)


def phase_body(y_ref, modes_ref, wave_ref):

    @pl.loop(0, 2)
    def _(b):
        places = cross(split(coordinates(y_ref[b]), 3), False).astype(BF16)
        columns = pl.ds(pl.multiple_of(b * 128, 128), 128)
        for r in range(0, 1024, 64):
            turns = nn(modes_ref[r : r + 64, :], places)
            rest = turns - jnp.round(turns)
            square = rest * rest
            wave_ref[r : r + 64, columns] = horner(COSTURN, square).astype(BF16)
            wave_ref[r + 1024 : r + 1088, columns] = (rest * horner(SINTURN, square)).astype(BF16)


def structure_body(odd_ref, w0, w1, w2, w3, q0, q1, q2, q3, mine_ref, theirs_ref):
    pieces = [jnp.concatenate(split(jnp.concatenate([q[0], q[1]], axis=1), 3), axis=0) for q in (q0, q1, q2, q3)]
    odd = odd_ref[...] == 1
    for i in range(2):
        halves = []
        for r in (i * 1024, i * 1024 + 512):
            s = None
            for p, w in zip(pieces, (w0, w1, w2, w3)):
                term = nt(p, w[r : r + 512, :])
                s = term if s is None else s + term
            halves.append(s[0:16] + s[16:32] + s[32:48])
        mine_ref[16 * i : 16 * i + 16, :] = jnp.where(odd, halves[1], halves[0])
        theirs_ref[16 * i : 16 * i + 16, :] = jnp.where(odd, halves[0], halves[1])


def respond_body(scale, scal_ref, w0, w1, w2, w3, q0, q1, q2, q3, mine_ref, theirs_ref, modes_ref, out_ref):
    k = modes_ref[...]
    square = k[0:1] * k[0:1] + k[1:2] * k[1:2] + k[2:3] * k[2:3]
    weight = scale * jnp.exp(square * -0.125) / (square + 1.0)
    low = jnp.where(scal_ref[ODD] == 0, mine_ref[...], theirs_ref[...])
    high = jnp.where(scal_ref[ODD] == 0, theirs_ref[...], mine_ref[...])
    total = jnp.concatenate([low, high], axis=1) * weight
    real, imag = total[0:16], total[16:32]
    left = [real] + [imag * k[j : j + 1] for j in range(3)]
    right = [imag] + [real * -k[j : j + 1] for j in range(3)]
    both = jnp.concatenate([jnp.concatenate(left, axis=0), jnp.concatenate(right, axis=0)], axis=1)
    pieces = jnp.concatenate(split(both, 2), axis=0)
    for i, (w, q) in enumerate(zip((w0, w1, w2, w3), (q0, q1, q2, q3))):
        out = nn(pieces, w[...])
        out = out[0:64] + out[64:128]
        for b in range(2):
            mine = out[:, b * 128 : (b + 1) * 128]
            force = [-jnp.sum(mine[16 * j + 16 : 16 * j + 32] * q[b], axis=0, keepdims=True) for j in range(3)]
            out_ref[scal_ref[PLACE + 2 * i + b]] = jnp.concatenate([mine[0:16]] + force + [jnp.zeros((5, 128), F32)], axis=0)


def finish_body(parts_ref, potential_ref, forces_ref):
    total = parts_ref[0]
    for i in range(1, 8):
        total = total + parts_ref[i]
    potential_ref[...] = total[0:16]
    forces_ref[...] = total[16:19]


def pairs(n_slab, target):
    return [(s * 8 + k, (target(s, k)[0] % n_slab) * 8 + target(s, k)[1]) for s in range(n_slab) for k in range(8)]


def move(x, target):
    return lax.ppermute(x, AXES, pairs(lax.axis_size("slab"), target))


def over_chip(s):
    return s + 1 if s % 2 else s - 1


def near_blocks(block, wide):
    half = move(wide, lambda s, k: (s, k ^ 1))
    near = move(block, lambda s, k: (over_chip(s), k))
    both = move(block, lambda s, k: (over_chip(s), k ^ 1))
    return half, near, both


def along_y(block, near, name, after):
    stack = call(stack_body, jax.ShapeDtypeStruct((4,) + block.shape, BF16), block, *near, name=name, after=after)
    return [stack] + [move(stack, lambda s, k, j=j: (s, (k - 2 * j) % 8)) for j in range(1, 4)]


def other_core(y):
    return move(y[0:2], lambda s, k: (s ^ 1, k))


def other_core_after(y, name, after):
    pair = call(pair_body, jax.ShapeDtypeStruct((2,) + y.shape[1:], BF16), y, name=name, after=after)
    return move(pair, lambda s, k: (s ^ 1, k))


def shards(
    atom_descriptors,
    atom_locations,
    adjacent_atom_slots,
    neighbour_tally,
    filled_slot_tallies,
    reciprocal_lattice_modes,
    edge_update_matrix,
    node_update_matrix,
    distance_basis_mixing,
    latent_ionic_readout,
):
    n_slab = lax.axis_size("slab")
    shape = jax.ShapeDtypeStruct
    where = jnp.stack([lax.axis_index("slab"), lax.axis_index("kgrp")]).astype(jnp.int32)
    block, with_slots = call(
        pack_body, (shape((PAYLOAD, ROWS), BF16), shape((WIDE, ROWS), BF16)),
        atom_descriptors, atom_locations, adjacent_atom_slots.T, neighbour_tally.reshape(1, ROWS), name="pack", limit=56,
    )
    near = near_blocks(block, with_slots)
    smem = pl.BlockSpec(memory_space=pltpu.SMEM)
    scal, shift, odd = call(
        layout_body, (shape((16,), jnp.int32), shape((3,), F32), shape((1, 512), jnp.int32)),
        scalars=(where, filled_slot_tallies), name="layout", out_specs=(smem, smem, pl.BlockSpec(memory_space=pltpu.VMEM)),
    )

    def count(source, which, name):
        return call(
            functools.partial(count_body, which), [shape((6, ROWS, 128), F32)] * 4, source, scalars=(scal,), name=name, flops=10**9
        )

    counts = count(with_slots, BASE, "counts")
    ys = along_y(block, near, "stack_first", (counts[0],))
    cs = [other_core(ys[0])]
    partner_counts = count(near[0], BASE_PARTNER, "partner_counts")
    wide = shape((8 * ROWS, 6 * ROWS), BF16)
    here = pltpu.VMEM((3, ROWS, 128), F32)
    message = lambda *n: pltpu.VMEM(n + (6 * ROWS, 128), BF16)
    basis = [None] * 4
    basis[0], part = call(
        first_body, (wide, shape((ROWS, 128), F32)),
        ys[0], cs[0], counts[0], edge_update_matrix, distance_basis_mixing,
        scalars=(shift,), name="first_0", flops=10**9, scratch=[here, message()],
    )
    cs += [other_core_after(ys[1], "pair_first", (part, partner_counts[0])), other_core(ys[2]), other_core(ys[3])]
    basis[1], basis[2], basis[3], hidden = call(
        first_rest_body, (wide, wide, wide, shape((ROWS, 128), BF16)),
        *ys, *cs[1:], *counts[1:], edge_update_matrix, distance_basis_mixing, part, node_update_matrix,
        scalars=(shift,), name="first_rest", flops=10**9, scratch=[here, message(3), pltpu.VMEM((ROWS, 128), F32)],
    )
    turns = call(modes_body, shape((1024, 24), BF16), reciprocal_lattice_modes, name="modes")

    def phases(j, after):
        return call(phase_body, shape((2048, 256), BF16), ys[j], turns, name=f"phases_{j}", flops=10**9, after=after)

    def partner_basis(a, b, after):
        return call(
            partner_body, [wide, wide], ys[0], ys[a], ys[b], cs[a], cs[b], partner_counts[a], partner_counts[b],
            scalars=(shift,), name=f"partner_{a}", flops=10**9, scratch=[here], after=after,
        )

    near = near_blocks(hidden, hidden)
    partner = [*partner_basis(0, 1, (hidden,))]
    waves = [phases(0, (hidden,))]
    ms = along_y(hidden, near, "stack_second", (partner[0], waves[0]))
    ns = [other_core(ms[0])]
    partner += [*partner_basis(2, 3, (ms[0],))]
    waves += [phases(1, (ms[0],))]
    part = call(
        second_body, shape((2, ROWS, 128), F32),
        ms[0], ns[0], basis[0], partner[0], edge_update_matrix, distance_basis_mixing,
        name="second_0", flops=10**9, scratch=[message()],
    )
    ns += [other_core_after(ms[1], "pair_second", (part, partner[2], *waves)), other_core(ms[2]), other_core(ms[3])]
    charges = call(
        second_rest_body, shape((2, 16, ROWS), F32),
        *ms[1:], *ns[1:], *basis[1:], *partner[1:], edge_update_matrix, distance_basis_mixing, part, ms[0], node_update_matrix, latent_ionic_readout.T,
        scalars=(scal,), name="second_rest", flops=10**9, scratch=[message(3), pltpu.VMEM((2, ROWS, 128), F32)],
    )
    qs = [charges] + [move(charges, lambda s, k, j=j: (s, (k - 2 * j) % 8)) for j in range(1, 4)]
    waves += [phases(j, (charges,)) for j in range(2, 4)]
    part, away = call(
        structure_body, (shape((32, 512), F32), shape((32, 512), F32)), odd, *waves, *qs,
        name="structure", flops=10**8,
    )
    part = part + move(away, lambda s, k: (s ^ 1, k))
    half = part.astype(BF16)
    part = part + sum(move(half, lambda s, k, m=m: (s + 8 * m, k)).astype(F32) for m in (1, 2, 3))
    half = part.astype(BF16)
    part = part + sum(move(half, lambda s, k, m=m: (s ^ (2 * m), k)).astype(F32) for m in (1, 2, 3))
    other = move(part, lambda s, k: (s ^ 1, k))
    scale = 4.0 / math.sqrt(n_slab * 1024 * reciprocal_lattice_modes.shape[1] * 8)
    partial = call(
        functools.partial(respond_body, scale), shape((8, 24, ROWS), F32), *waves, *qs, part, other, reciprocal_lattice_modes,
        scalars=(scal,), name="respond", flops=10**8,
    )
    partial = lax.all_to_all(partial, "kgrp", 0, 0)
    return tuple(call(finish_body, (shape((16, ROWS), F32), shape((3, ROWS), F32)), partial, name="finish"))


def solution(mesh):
    return jax.shard_map(
        shards,
        mesh=mesh,
        in_specs=(
            P(("slab", "kgrp"), None),
            P(None, ("slab", "kgrp")),
            P(("slab", "kgrp"), None),
            P(("slab", "kgrp")),
            P(),
            P(None, "kgrp"),
            P(),
            P(),
            P(),
            P(),
        ),
        out_specs=(P(None, ("slab", "kgrp")), P(None, ("slab", "kgrp"))),
        check_vma=False,
    )
```
